1024 devices in a mesh: dp: 16 (over y, core), expert: 64 (over x, z).
Axes of the slice: x: 4, y: 8, z: 16, core: 2. Of those that a mesh axis runs over, the one named last changes fastest.
Arguments:
- tokens: bfloat16 [16384, 2048], P(('dp', 'expert')), may hold values from -6 to 6
- expert_ids: int32 [16384, 8], P(('dp', 'expert')), may hold values from 0 to 63, all different within a row; in each aligned block of 16 rows (0 to 15, 16 to 31, ...) at most 4 rows name the same one
- route_weights: bfloat16 [16384, 8], P(('dp', 'expert')), may hold values from 0.049804688 to 0.5
- out_grad: bfloat16 [16384, 2048], P(('dp', 'expert')), may hold values from -6 to 6
- w_gate: bfloat16 [64, 2048, 384], P('expert'), may hold values from -0.125 to 0.125
- w_up: bfloat16 [64, 2048, 384], P('expert'), may hold values from -0.125 to 0.125
- w_down: bfloat16 [64, 384, 2048], P('expert'), may hold values from -0.3125 to 0.3125
Outputs:
- grad_tokens: bfloat16 [16384, 2048], P(('dp', 'expert'))
- grad_route: bfloat16 [16384, 8], P(('dp', 'expert'))
- grad_gate: float32 [64, 2048, 384], P('expert', 'dp')
- grad_up: float32 [64, 2048, 384], P('expert', 'dp')
- grad_down: float32 [64, 384, 2048], P('expert', None, 'dp')
The draws below stay inside these ranges and needn't reach their ends.
Inputs may be any that keep to these rules, and one draw needn't show every extreme that they name: `expert_ids`: each token names 8 different experts. Among the 16 tokens of one device no expert is named more than 4 times, and in every draw some device names some expert exactly 4 times.
All inputs are finite; a program needn't handle non-finite values.
Results may differ from the reference program's by a relative error of at most 0.02.
Values may be sent and summed in bfloat16 or wider, within the bound.
No kernel may reach another device: no remote copies, remote signals or barrier semaphores. Data moves between devices by JAX's collectives and lax.ppermute only.
A program may use at most 32 MiB of HBM per device.

```python
import math
import jax
import jax.numpy as jnp
import numpy as np
from jax import lax

D = 2048
FF = 384
TOP = 8
TOK_DEV = 16
EXPERTS = 64
CAP = 4
TOKENS = 16384
N_DP = 16
N_EXPERT = 64


def strengthened(values, rng, source, target, parts, factor):
    def block_of(axis_at):
        return (jnp.arange(values.shape[axis_at]) // (values.shape[axis_at] // parts)).reshape((-1,) + (1,) * (values.ndim - 1 - axis_at))

    one_side = jax.random.permutation(rng, parts)[block_of(target)]
    far = (block_of(target) + parts // 2) % parts
    return jnp.where((block_of(source) == one_side) | (block_of(source) == far), factor * values, values)


def level_of(key, extent, shards, smallest, top_value):
    gain, own = 1.0, jax.random.fold_in(key, 6)
    for axis_at, parts in shards:
        steps = jnp.exp(jax.random.uniform(jax.random.fold_in(own, axis_at), (parts,), jnp.float32, smallest / len(shards), top_value / len(shards)))
        gain = gain * jnp.repeat(steps, extent[axis_at] // parts).reshape([-1 if axis == axis_at else 1 for axis in range(len(extent))])
    return gain


def routed_block(rng, own, number, rows, count, top, bound, skew):
    order = jax.random.permutation(rng, count)
    packed, ordinary = shares(count, rows * top, bound, skew, True), shares(count, rows * top, bound, skew, False)
    places = jnp.arange(count)

    def named(lengths, offset_by):
        used = int((lengths > 0).sum())
        fixed = max(1, used // 4)
        moved = fixed + (places - fixed + offset_by * (used - fixed)) % max(1, count - fixed)
        return jnp.zeros((count,), jnp.int32).at[order[jnp.where(places < fixed, places, moved)]].set(jnp.asarray(lengths, jnp.int32))

    lengths = jnp.where(number % 4 == 0, named(packed, number // 4), named(ordinary, number - number // 4 - 1))
    mixed = jax.random.permutation(jax.random.fold_in(own, 3), count)
    giver, receiver = mixed[0:count // 2 * 2:2], mixed[1:count // 2 * 2:2]
    margin = jnp.minimum(lengths[giver] - 1, bound - lengths[receiver]) // 2
    margin = jnp.where((giver == order[0]) | (receiver == order[0]) | (lengths[receiver] == 0), 0, jnp.maximum(margin, 0))
    moved = jax.random.randint(jax.random.fold_in(own, 4), (count // 2,), 0, 1 << 20) % (margin + 1)
    lengths = lengths.at[giver].add(-moved).at[receiver].add(moved)
    labels = jnp.searchsorted(jnp.cumsum(lengths), jnp.arange(rows * top), side="right").astype(jnp.int32)
    listing = labels.reshape(top, rows).T
    listing = listing[jax.random.permutation(jax.random.fold_in(own, 1), rows)]
    offset_by = jax.random.randint(jax.random.fold_in(own, 2), (rows, 1), 0, top)
    return jnp.take_along_axis(listing, (jnp.arange(top)[None, :] + offset_by) % top, axis=1)


def shares(amount, total, bound, lean, full):
    weights = [(1 << 20) // math.isqrt(grade ** lean) + 1 for grade in range(1, amount + 1)]
    largest = bound if full else min(bound, max(-(-total // amount), total * weights[0] // sum(weights)))
    least = 1 if total - largest >= amount - 1 else 0
    counts, surplus = [largest] + [least] * (amount - 1), total - largest - least * (amount - 1)
    while surplus > 0:
        movable = [i for i in range(1, amount) if counts[i] < largest] or [i for i in range(1, amount) if counts[i] < bound]
        pool, left = sum([weights[i] for i in movable]), surplus
        for i in movable:
            addition = min(bound - counts[i], max(1, left * weights[i] // pool), surplus)
            counts[i] = counts[i] + addition
            surplus = surplus - addition
    return np.array(counts)


def noise(stream_key, extent, spread, limit, split=(), kind=jnp.bfloat16):
    values = jax.random.normal(stream_key, extent, jnp.float32) * spread
    if len(split) > 0:
        values = level_of(stream_key, extent, split, -0.22, 0.18) * values
    return jnp.clip(values, min=-limit, max=limit).astype(kind)


def heavy_noise(stream_key, dims, spread, reach, shards, heavy, kind=jnp.bfloat16):
    entries = spread * jax.random.normal(stream_key, dims, jnp.float32)
    if shards:
        entries = entries * level_of(stream_key, dims, shards, -0.22, 0.18)
    return jnp.clip(strengthened(entries, jax.random.fold_in(stream_key, 3), *heavy), -reach, reach).astype(kind)


def setup_inputs(seed: int = 0) -> dict:
    key_list = jax.random.split(jax.random.key(seed), 8)
    tokens = noise(key_list[0], (TOKENS, D), 1.0, 6.0, ((0, 1024),))
    expert_ids_keys = jax.random.split(jax.random.fold_in(key_list[1], 1), TOKENS // TOK_DEV)
    expert_ids_turns = jax.random.permutation(jax.random.fold_in(key_list[1], 3), TOKENS // TOK_DEV)
    expert_ids = jax.vmap(lambda own, number: routed_block(jax.random.fold_in(key_list[1], 2), own, number, TOK_DEV, EXPERTS, TOP, CAP, 2))(expert_ids_keys, expert_ids_turns).reshape((TOKENS, TOP))
    route_weights = jnp.clip(jnp.exp(math.log(0.5) - 2.306499 * jax.random.uniform(key_list[2], (TOKENS, TOP), jnp.float32) ** level_of(key_list[2], (TOKENS, TOP), ((0, 1024),), -0.2, 0.2)), 0.049804688, 0.5).astype(jnp.bfloat16)
    out_grad = heavy_noise(key_list[3], (TOKENS, D), 0.25, 6.0, ((0, 1024),), (0, 1, 1024, 6.0))
    w_gate = noise(key_list[4], (EXPERTS, D, FF), D ** -0.5, 0.125, ((0, 64),))
    w_up = noise(key_list[5], (EXPERTS, D, FF), D ** -0.5, 0.125, ((0, 64),))
    w_down = noise(key_list[6], (EXPERTS, FF, D), FF ** -0.5, 0.3125, ((0, 64),))
    return {"tokens": tokens, "expert_ids": expert_ids, "route_weights": route_weights, "out_grad": out_grad, "w_gate": w_gate, "w_up": w_up, "w_down": w_down}


def slot_positions(flat_ids):
    onehot = (flat_ids[:, None] == jnp.arange(EXPERTS, dtype=jnp.int32)[None, :]).astype(jnp.int32)
    running = jnp.cumsum(onehot, axis=0)
    return jnp.sum(onehot * (running - 1), axis=1).astype(jnp.int32)


def rounded(value):
    low = value.astype(jnp.bfloat16)
    low = lax.optimization_barrier(low)
    return low.astype(jnp.float32)


def reference(tokens, expert_ids, route_weights, out_grad, w_gate, w_up, w_down):
    routed = TOK_DEV * TOP
    slots = N_EXPERT * CAP
    gate32 = w_gate.astype(jnp.float32)
    up32 = w_up.astype(jnp.float32)
    down32 = w_down.astype(jnp.float32)
    tok = tokens.reshape(N_DP, N_EXPERT, TOK_DEV, D)
    ids = expert_ids.reshape(N_DP, N_EXPERT, routed).astype(jnp.int32)
    wts = route_weights.reshape(N_DP, N_EXPERT, routed)
    cot = out_grad.reshape(N_DP, N_EXPERT, TOK_DEV, D)
    source = jnp.arange(N_EXPERT, dtype=jnp.int32)[:, None]

    def group(totals, inputs):
        g_tok, g_ids, g_wts, g_cot = inputs
        pos = jax.vmap(slot_positions)(g_ids)
        col = (source * CAP + pos).astype(jnp.int32)
        x_rows = jnp.repeat(g_tok, TOP, axis=1)
        y_rows = jnp.repeat(g_cot, TOP, axis=1)
        xs = jnp.zeros((EXPERTS, slots, D), jnp.bfloat16).at[g_ids, col].set(x_rows)
        ys = jnp.zeros((EXPERTS, slots, D), jnp.bfloat16).at[g_ids, col].set(y_rows)
        ws = jnp.zeros((EXPERTS, slots), jnp.bfloat16).at[g_ids, col].set(g_wts)
        x32 = xs.astype(jnp.float32)
        y32 = ys.astype(jnp.float32)
        g32 = (ws.astype(jnp.float32)[..., None] * y32).astype(jnp.bfloat16).astype(jnp.float32)
        pre_gate = jnp.einsum('esd,edf->esf', x32, gate32)
        pre_up = jnp.einsum('esd,edf->esf', x32, up32)
        sigma = jax.nn.sigmoid(pre_gate)
        hidden = (pre_gate * sigma * pre_up).astype(jnp.bfloat16).astype(jnp.float32)
        output = jnp.einsum('esf,efd->esd', hidden, down32)
        route_term = jnp.sum(output * y32, axis=2).astype(jnp.bfloat16)
        back_hidden = jnp.einsum('esd,efd->esf', g32, down32)
        gate_back = (back_hidden * pre_up * sigma * (1.0 + pre_gate * (1.0 - sigma))).astype(jnp.bfloat16).astype(jnp.float32)
        up_back = (back_hidden * pre_gate * sigma).astype(jnp.bfloat16).astype(jnp.float32)
        grad_in = (jnp.einsum('esf,edf->esd', gate_back, gate32) + jnp.einsum('esf,edf->esd', up_back, up32)).astype(jnp.bfloat16)
        part_gate = rounded(jnp.einsum('esd,esf->edf', x32, gate_back))
        part_up = rounded(jnp.einsum('esd,esf->edf', x32, up_back))
        part_down = rounded(jnp.einsum('esf,esd->efd', hidden, g32))
        totals = (totals[0] + part_gate, totals[1] + part_up, totals[2] + part_down)
        back_rows = grad_in[g_ids, col].astype(jnp.float32).reshape(N_EXPERT, TOK_DEV, TOP, D)
        token_grad = jnp.sum(back_rows, axis=2).astype(jnp.bfloat16)
        route_grad = route_term[g_ids, col].reshape(N_EXPERT, TOK_DEV, TOP)
        return totals, (token_grad, route_grad)

    start = (jnp.zeros((EXPERTS, D, FF), jnp.float32), jnp.zeros((EXPERTS, D, FF), jnp.float32), jnp.zeros((EXPERTS, FF, D), jnp.float32))
    totals, per_token = lax.scan(group, start, (tok, ids, wts, cot))
    scale = 1.0 / N_DP
    grad_tokens = per_token[0].reshape(TOKENS, D)
    grad_route = per_token[1].reshape(TOKENS, TOP)
    return grad_tokens, grad_route, totals[0] * scale, totals[1] * scale, totals[2] * scale
```

```python
import jax
import jax.numpy as jnp
from jax import lax
from jax.sharding import Mesh
from jax.sharding import PartitionSpec as P

BF = jnp.bfloat16
F32 = jnp.float32
META = 128
FIRST = (((0,), (0,)), ((), ()))
LAST = (((1,), (1,)), ((), ()))


def shards(tokens, expert_ids, route_weights, out_grad, w_gate, w_up, w_down):
    tok, width = tokens.shape
    top = expert_ids.shape[1]
    nx, nh, nl = lax.axis_size("x"), lax.axis_size("zh"), lax.axis_size("zl")
    ny, nc = lax.axis_size("y"), lax.axis_size("core")
    experts = nx * nh * nl
    cap = min(tok, max(2, 2 * tok * top // experts))
    held = nh * tok
    dests = nx * nl
    per = nh * cap
    slots = dests * per

    meta = jnp.concatenate(
        [
            expert_ids.astype(BF),
            route_weights,
            jnp.zeros((tok, META - 2 * top), BF),
        ],
        axis=1,
    )
    packed = jnp.concatenate([tokens, out_grad, meta], axis=1)
    gathered = lax.all_gather(packed, "zh", axis=0, tiled=True)
    rows = gathered[:, :width]
    cots = gathered[:, width : 2 * width]
    ids = gathered[:, 2 * width : 2 * width + top].astype(jnp.int32)
    weights = gathered[:, 2 * width + top : 2 * width + 2 * top].astype(F32)

    dest = jnp.arange(dests, dtype=jnp.int32)
    dest_ids = (dest // nl) * (nh * nl) + lax.axis_index("zh") * nl + dest % nl
    named = ids[None, :, :] == dest_ids[:, None, None]
    match = jnp.any(named, axis=2)
    weight_of = jnp.sum(jnp.where(named, weights[None], 0.0), axis=2)
    t = jnp.arange(held, dtype=jnp.int32)
    earlier = ((t[:, None] < t[None, :]) & (t[:, None] // tok == t[None, :] // tok)).astype(BF)
    position = jnp.dot(match.astype(BF), earlier, preferred_element_type=F32).astype(jnp.int32)
    place = (t // tok) * cap + position
    select = (
        match[:, None, :] & (place[:, None, :] == jnp.arange(per, dtype=jnp.int32)[None, :, None])
    )
    pick = select.astype(BF).reshape(slots, held)
    scaled_pick = jnp.where(select, weight_of[:, None, :], 0.0).astype(BF).reshape(slots, held)
    send_rows = jnp.dot(pick, rows, preferred_element_type=F32).astype(BF)
    send_cots = jnp.dot(scaled_pick, cots, preferred_element_type=F32).astype(BF)

    def forward(a):
        return lax.all_to_all(
            a.reshape(dests, per, -1), ("x", "zl"), split_axis=0, concat_axis=0, tiled=True
        ).reshape(slots, -1)

    inputs = forward(send_rows)
    scaled = forward(send_cots)

    gate_w, up_w, down_w = w_gate[0], w_up[0], w_down[0]
    pre_gate = jnp.dot(inputs, gate_w, preferred_element_type=F32)
    pre_up = jnp.dot(inputs, up_w, preferred_element_type=F32)
    sigma = jax.nn.sigmoid(pre_gate)
    hidden = (pre_gate * sigma * pre_up).astype(BF)
    back_hidden = lax.dot_general(scaled, down_w, LAST, preferred_element_type=F32)
    weighted_route = jnp.sum(hidden.astype(F32) * back_hidden, axis=1, keepdims=True)
    gate_back = (back_hidden * pre_up * sigma * (1.0 + pre_gate * (1.0 - sigma))).astype(BF)
    up_back = (back_hidden * pre_gate * sigma).astype(BF)

    part = jnp.stack(
        [
            lax.dot_general(inputs, gate_back, FIRST, preferred_element_type=F32).astype(BF),
            lax.dot_general(inputs, up_back, FIRST, preferred_element_type=F32).astype(BF),
            lax.dot_general(scaled, hidden, FIRST, preferred_element_type=F32).astype(BF),
        ]
    )
    block = width // (ny * nc)
    ff = part.shape[2]
    part = part.reshape(3, ny, nc, block, ff)
    core = lax.axis_index("core")
    other = lax.dynamic_index_in_dim(part, 1 - core, 2, keepdims=False)
    own = lax.dynamic_index_in_dim(part, core, 2, keepdims=False)
    came = lax.ppermute(other, "core", [(0, 1), (1, 0)])
    pair = (own.astype(F32) + came.astype(F32)).astype(BF)
    pair = pair.transpose(1, 0, 2, 3).reshape(ny * 3 * block, ff)
    total = lax.psum_scatter(pair, "y", scatter_dimension=0, tiled=True)
    total = total.reshape(3, block, ff).astype(F32) * (1.0 / (ny * nc))

    grad_in = lax.dot_general(gate_back, gate_w, LAST, preferred_element_type=F32)
    grad_in = (
        grad_in + lax.dot_general(up_back, up_w, LAST, preferred_element_type=F32)
    ).astype(BF)
    high = weighted_route.astype(BF)
    low = (weighted_route - high.astype(F32)).astype(BF)
    back = jnp.concatenate([grad_in, high, low, jnp.zeros((slots, META - 2), BF)], axis=1)
    back = forward(back)
    token_part = lax.dot_general(
        pick, back[:, :width], FIRST, preferred_element_type=F32
    ).astype(BF)
    route_rows = back[:, width].astype(F32) + back[:, width + 1].astype(F32)
    by_dest = jnp.sum(
        jnp.where(select, route_rows.reshape(dests, per)[:, :, None], 0.0), axis=1
    )
    route_part = jnp.sum(jnp.where(named, by_dest[:, :, None], 0.0), axis=0) / weights
    outgoing = jnp.concatenate(
        [token_part, route_part.astype(BF), jnp.zeros((held, META - top), BF)], axis=1
    )
    parts = lax.all_to_all(
        outgoing.reshape(nh, tok, -1), "zh", split_axis=0, concat_axis=0, tiled=True
    )
    summed = jnp.sum(parts.astype(F32), axis=0)
    grad_tokens = summed[:, :width].astype(BF)
    grad_route = summed[:, width : width + top].astype(BF)
    return (grad_tokens, grad_route, total[0][None], total[1][None], total[2].T[None])


def solution(mesh):
    groups, experts = mesh.devices.shape
    n = round(experts ** (1 / 3))
    fine = Mesh(
        mesh.devices.reshape(groups // 2, 2, n, n, n), ("y", "core", "x", "zh", "zl")
    )
    dp = ("y", "core")
    ex = ("x", "zh", "zl")
    rows = P(dp + ex, None)
    return jax.shard_map(
        shards,
        mesh=fine,
        in_specs=(rows, rows, rows, rows) + (P(ex, None, None),) * 3,
        out_specs=(rows, rows, P(ex, dp, None), P(ex, dp, None), P(ex, None, dp)),
        check_vma=False,
    )
```

```python
import functools

import jax
import jax.numpy as jnp
from jax import lax
from jax.experimental import pallas as pl
from jax.experimental.pallas import tpu as pltpu
from jax.sharding import Mesh
from jax.sharding import PartitionSpec as P

BF = jnp.bfloat16
F32 = jnp.float32
META = 128
VMEM = pl.BlockSpec(memory_space=pltpu.VMEM)
FIRST = (((0,), (0,)), ((), ()))
LAST = (((1,), (1,)), ((), ()))


def call(body, outs, flops, moved):
    return pl.pallas_call(
        body,
        out_shape=outs,
        compiler_params=pltpu.CompilerParams(vmem_limit_bytes=30 * 1024 * 1024),
        cost_estimate=pl.CostEstimate(flops=flops, bytes_accessed=moved, transcendentals=0),
    )


def select_body(tok, cap, top, held_ref, dest_ref, send_ref, pick_ref):
    held = held_ref.shape[0]
    slots, width = send_ref.shape[0], send_ref.shape[1] // 2
    meta = held_ref[:, 2 * width :].astype(F32)
    dest = dest_ref[...]
    match = jnp.zeros((held, slots), F32)
    weight = jnp.zeros((held, slots), F32)
    for k in range(top):
        same = meta[:, k : k + 1] == dest
        match = jnp.where(same, 1.0, match)
        weight = jnp.where(same, meta[:, top + k : top + k + 1], weight)
    row = lax.broadcasted_iota(jnp.int32, (held, held), 0)
    col = lax.broadcasted_iota(jnp.int32, (held, held), 1)
    earlier = jnp.where((col < row) & (col // tok == row // tok), 1.0, 0.0).astype(BF)
    position = jnp.dot(earlier, match.astype(BF), preferred_element_type=F32).astype(jnp.int32)
    token = lax.broadcasted_iota(jnp.int32, (held, slots), 0)
    slot = lax.broadcasted_iota(jnp.int32, (held, slots), 1) % (held // tok * cap)
    pick = (match > 0.5) & (position + token // tok * cap == slot) & (position < cap)
    flat = jnp.where(pick, 1.0, 0.0).astype(BF)
    scaled = jnp.where(pick, weight, 0.0).astype(BF)
    pick_ref[...] = flat
    for half, chosen in ((0, flat), (1, scaled)):
        send_ref[:, half * width : (half + 1) * width] = lax.dot_general(
            chosen,
            held_ref[:, half * width : (half + 1) * width],
            FIRST,
            preferred_element_type=F32,
        ).astype(BF)


def expert_body(nblock, core_ref, came_ref, gate_ref, up_ref, down_ref, hidden_ref, gate_back_ref, up_back_ref, route_ref, other_ref):
    width = came_ref.shape[1] // 2
    inputs, scaled = came_ref[:, :width], came_ref[:, width:]
    pre_gate = jnp.dot(inputs, gate_ref[...], preferred_element_type=F32)
    pre_up = jnp.dot(inputs, up_ref[...], preferred_element_type=F32)
    back_hidden = lax.dot_general(scaled, down_ref[...], LAST, preferred_element_type=F32)
    sigma = 1.0 / (1.0 + jnp.exp(-pre_gate))
    active = pre_gate * sigma
    hidden = (active * pre_up).astype(BF)
    gate_back = (back_hidden * pre_up * sigma * (1.0 + pre_gate * (1.0 - sigma))).astype(BF)
    up_back = (back_hidden * active).astype(BF)
    hidden_ref[...] = hidden
    gate_back_ref[...] = gate_back
    up_back_ref[...] = up_back
    route = jnp.sum(hidden.astype(F32) * back_hidden, axis=1, keepdims=True)
    high = route.astype(BF).astype(F32)
    lane = lax.broadcasted_iota(jnp.int32, route_ref.shape, 1)
    route_ref[...] = jnp.where(
        lane == 0, high, jnp.where(lane == 1, route - high, 0.0)
    ).astype(BF)
    weight_terms(nblock, 1 - core_ref[0], came_ref, hidden, gate_back, up_back, None, other_ref)


def weight_terms(nblock, core, came_ref, hidden, gate_back, up_back, add_ref, out_ref):
    width = came_ref.shape[1] // 2
    block = width // nblock
    for y in range(nblock // 2):
        for which, (base, right) in enumerate(
            ((0, gate_back), (0, up_back), (width, hidden))
        ):
            at = pl.multiple_of(base + (2 * y + core) * block, block)
            term = lax.dot_general(
                came_ref[:, pl.ds(at, block)], right, FIRST, preferred_element_type=F32
            )
            if add_ref is not None:
                term = term + add_ref[y, which].astype(F32)
            out_ref[y, which] = term.astype(BF)


def own_body(nblock, core_ref, came_ref, hidden_ref, gate_back_ref, up_back_ref, add_ref, out_ref):
    weight_terms(
        nblock, core_ref[0], came_ref, hidden_ref[...], gate_back_ref[...], up_back_ref[...], add_ref, out_ref
    )


def back_body(gate_back_ref, up_back_ref, route_ref, gate_ref, up_ref, out_ref):
    width = gate_ref.shape[0]
    out = lax.dot_general(gate_back_ref[...], gate_ref[...], LAST, preferred_element_type=F32)
    out = out + lax.dot_general(up_back_ref[...], up_ref[...], LAST, preferred_element_type=F32)
    out_ref[:, :width] = out.astype(BF)
    out_ref[:, width:] = route_ref[...]


def combine_body(top, back_ref, pick_ref, meta_ref, dest_ref, out_ref):
    width = back_ref.shape[1] - META
    pick = pick_ref[...]
    out_ref[:, :width] = jnp.dot(pick, back_ref[:, :width], preferred_element_type=F32).astype(BF)
    lane8 = lax.broadcasted_iota(jnp.int32, (8, META), 1)
    pair = jnp.where(lane8 < 2, 1.0, 0.0).astype(BF)
    route = lax.dot_general(pair, back_ref[:, width:], LAST, preferred_element_type=F32)[0:1]
    mine = jnp.where(pick.astype(F32) > 0.5, route, 0.0)
    meta = meta_ref[...].astype(F32)
    dest = dest_ref[...]
    lane = lax.broadcasted_iota(jnp.int32, (pick.shape[0], META), 1)
    routes = jnp.zeros((pick.shape[0], META), F32)
    for k in range(top):
        value = jnp.sum(
            jnp.where(meta[:, k : k + 1] == dest, mine, 0.0), axis=1, keepdims=True
        )
        routes = jnp.where(lane == k, value / meta[:, top + k : top + k + 1], routes)
    out_ref[:, width:] = routes.astype(BF)


def shards(tokens, expert_ids, route_weights, out_grad, w_gate, w_up, w_down):
    tok, width = tokens.shape
    top = expert_ids.shape[1]
    ff = w_gate.shape[2]
    nx, nh, nl = lax.axis_size("x"), lax.axis_size("zh"), lax.axis_size("zl")
    ny, nc = lax.axis_size("y"), lax.axis_size("core")
    nz = nh * nl
    experts = nx * nz
    cap = min(tok, max(2, 2 * tok * top // experts))
    held = nh * tok
    dests = nx * nl
    per = nh * cap
    slots = dests * per
    nblock = ny * nc
    block = width // nblock

    shift = nl // 2
    groups = [
        [(c * nx + x) * nz + (b * nl + c * shift + l) % nz for x in range(nx) for l in range(nl)]
        for c in range(nc)
        for b in range(nh)
    ]
    core = lax.axis_index("core")
    z = lax.axis_index("zh") * nl + lax.axis_index("zl")
    first = (z - core * shift + nz) % nz // nl * nl + core * shift
    dest = jnp.arange(slots, dtype=jnp.int32) // per
    dest_ids = (dest // nl) * nz + (first + dest % nl) % nz
    dest_ids = dest_ids.astype(F32).reshape(1, slots)
    core_at = core.reshape(1).astype(jnp.int32)

    def forward(a):
        return lax.all_to_all(
            a.reshape(dests, per, -1),
            ("core", "x", "zh", "zl"),
            split_axis=0,
            concat_axis=0,
            tiled=True,
            axis_index_groups=groups,
        ).reshape(slots, -1)

    meta = jnp.concatenate(
        [
            expert_ids.astype(BF),
            route_weights,
            jnp.zeros((tok, META - 2 * top), BF),
        ],
        axis=1,
    )
    packed = jnp.concatenate([tokens, out_grad, meta], axis=1)
    gathered = lax.all_gather(packed, "zh", axis=0, tiled=True)

    send, pick = call(
        functools.partial(select_body, tok, cap, top),
        (
            jax.ShapeDtypeStruct((slots, 2 * width), BF),
            jax.ShapeDtypeStruct((held, slots), BF),
        ),
        4 * slots * held * width,
        6 * slots * width,
    )(gathered, dest_ids)
    came = forward(send)

    gate_w, up_w, down_w = w_gate[0], w_up[0], w_down[0]
    small = jax.ShapeDtypeStruct((slots, ff), BF)
    terms = jax.ShapeDtypeStruct((ny, 3, block, ff), BF)
    smem = pl.BlockSpec(memory_space=pltpu.SMEM)
    hidden, gate_back, up_back, route, other = pl.pallas_call(
        functools.partial(expert_body, nblock),
        out_shape=(small, small, small, jax.ShapeDtypeStruct((slots, META), BF), terms),
        in_specs=[smem] + [VMEM] * 4,
        compiler_params=pltpu.CompilerParams(vmem_limit_bytes=40 * 1024 * 1024),
        cost_estimate=pl.CostEstimate(
            flops=9 * slots * ff * width, bytes_accessed=10_000_000, transcendentals=slots * ff
        ),
    )(core_at, came, gate_w, up_w, down_w)
    arrived = lax.ppermute(other, "core", [(0, 1), (1, 0)])
    back = call(
        back_body,
        jax.ShapeDtypeStruct((slots, width + META), BF),
        4 * slots * ff * width,
        5_000_000,
    )(gate_back, up_back, route, gate_w, up_w)
    pair = pl.pallas_call(
        functools.partial(own_body, nblock),
        out_shape=terms,
        in_specs=[smem] + [VMEM] * 5,
        compiler_params=pltpu.CompilerParams(vmem_limit_bytes=30 * 1024 * 1024),
        cost_estimate=pl.CostEstimate(
            flops=3 * slots * ff * width, bytes_accessed=7_000_000, transcendentals=0
        ),
    )(core_at, came, hidden, gate_back, up_back, arrived)
    total = lax.psum_scatter(
        pair.reshape(ny * 3 * block, ff), "y", scatter_dimension=0, tiled=True
    )
    total = total.reshape(3, block, ff).astype(F32) * (1.0 / (ny * nc))

    back = forward(back)
    outgoing = call(
        functools.partial(combine_body, top),
        jax.ShapeDtypeStruct((held, width + META), BF),
        2 * slots * held * width,
        2_000_000,
    )(back, pick, gathered[:, 2 * width :], dest_ids)
    parts = lax.all_to_all(
        outgoing.reshape(nh, tok, -1), "zh", split_axis=0, concat_axis=0, tiled=True
    )
    summed = jnp.sum(parts.astype(F32), axis=0)
    grad_tokens = summed[:, :width].astype(BF)
    grad_route = summed[:, width : width + top].astype(BF)
    return (grad_tokens, grad_route, total[0][None], total[1][None], total[2].T[None])


def solution(mesh):
    groups, experts = mesh.devices.shape
    n = round(experts ** (1 / 3))
    fine = Mesh(
        mesh.devices.reshape(groups // 2, 2, n, n, n), ("y", "core", "x", "zh", "zl")
    )
    dp = ("y", "core")
    ex = ("x", "zh", "zl")
    rows = P(dp + ex, None)
    return jax.shard_map(
        shards,
        mesh=fine,
        in_specs=(rows, rows, rows, rows) + (P(ex, None, None),) * 3,
        out_specs=(rows, rows, P(ex, dp, None), P(ex, dp, None), P(ex, None, dp)),
        check_vma=False,
    )
```

```python
import functools

import jax
import jax.numpy as jnp
from jax import lax
from jax.experimental import pallas as pl
from jax.experimental.pallas import tpu as pltpu
from jax.sharding import Mesh
from jax.sharding import PartitionSpec as P

BF = jnp.bfloat16
F32 = jnp.float32
META = 128
VMEM = pl.BlockSpec(memory_space=pltpu.VMEM)
APART = pl.BlockSpec(memory_space=pltpu.HBM)
FIRST = (((0,), (0,)), ((), ()))
LAST = (((1,), (1,)), ((), ()))


def call(body, outs, flops, moved, ins=None, scratch=(), limit=16, exps=0, out_specs=None):
    extra = {} if ins is None else {"in_specs": ins}
    if out_specs is not None:
        extra["out_specs"] = out_specs
    return pl.pallas_call(
        body,
        out_shape=outs,
        scratch_shapes=scratch,
        compiler_params=pltpu.CompilerParams(vmem_limit_bytes=limit * 1024 * 1024),
        cost_estimate=pl.CostEstimate(flops=flops, bytes_accessed=moved, transcendentals=exps),
        **extra,
    )


def pack_body(top, tokens_ref, cots_ref, ids_ref, weights_ref, out_ref, ids_here, weights_here, sems):
    width = tokens_ref.shape[1]
    copies = [
        pltpu.make_async_copy(source, target, sems.at[n])
        for n, (source, target) in enumerate(
            (
                (ids_ref, ids_here),
                (weights_ref, weights_here),
                (tokens_ref, out_ref.at[:, pl.ds(0, width)]),
                (cots_ref, out_ref.at[:, pl.ds(width, width)]),
            )
        )
    ]
    for copy in copies:
        copy.start()
    lane = lax.broadcasted_iota(jnp.int32, (top, META), 1)
    row = lax.broadcasted_iota(jnp.int32, (top, META), 0)
    copies[0].wait()
    copies[1].wait()
    meta = lax.dot_general(
        ids_here[...].astype(F32).astype(BF),
        jnp.where(lane == row, 1.0, 0.0).astype(BF),
        FIRST,
        preferred_element_type=F32,
    ) + lax.dot_general(
        weights_here[...].astype(F32).astype(BF),
        jnp.where(lane == row + top, 1.0, 0.0).astype(BF),
        FIRST,
        preferred_element_type=F32,
    )
    out_ref[:, 2 * width :] = meta.astype(BF)
    copies[2].wait()
    copies[3].wait()


def select_body(tok, cap, top, held_ref, dest_ref, send_ref, pick_ref, meta_ref):
    held = held_ref.shape[0]
    slots, width = send_ref.shape[0], send_ref.shape[1] // 2
    meta_ref[...] = held_ref[:, 2 * width :]
    meta = held_ref[:, 2 * width :].astype(F32)
    dest = dest_ref[...]
    match = jnp.zeros((held, slots), F32)
    weight = jnp.zeros((held, slots), F32)
    for k in range(top):
        same = meta[:, k : k + 1] == dest
        match = jnp.where(same, 1.0, match)
        weight = jnp.where(same, meta[:, top + k : top + k + 1], weight)
    row = lax.broadcasted_iota(jnp.int32, (held, held), 0)
    col = lax.broadcasted_iota(jnp.int32, (held, held), 1)
    earlier = jnp.where((col < row) & (col // tok == row // tok), 1.0, 0.0).astype(BF)
    position = jnp.dot(earlier, match.astype(BF), preferred_element_type=F32).astype(jnp.int32)
    token = lax.broadcasted_iota(jnp.int32, (held, slots), 0)
    slot = lax.broadcasted_iota(jnp.int32, (held, slots), 1) % (held // tok * cap)
    pick = (match > 0.5) & (position + token // tok * cap == slot) & (position < cap)
    flat = jnp.where(pick, 1.0, 0.0).astype(BF)
    scaled = jnp.where(pick, weight, 0.0).astype(BF)
    pick_ref[...] = flat
    for half, chosen in ((0, flat), (1, scaled)):
        send_ref[:, half * width : (half + 1) * width] = lax.dot_general(
            chosen,
            held_ref[:, half * width : (half + 1) * width],
            FIRST,
            preferred_element_type=F32,
        ).astype(BF)


def expert_body(
    nblock,
    core_ref,
    came_ref,
    gate_ref,
    up_ref,
    down_ref,
    hidden_ref,
    gate_back_ref,
    up_back_ref,
    route_ref,
    other_ref,
    buffer,
    sems,
):
    width = came_ref.shape[1] // 2
    inputs, scaled = came_ref[:, :width], came_ref[:, width:]
    pre_gate = jnp.dot(inputs, gate_ref[...], preferred_element_type=F32)
    pre_up = jnp.dot(inputs, up_ref[...], preferred_element_type=F32)
    back_hidden = lax.dot_general(scaled, down_ref[...], LAST, preferred_element_type=F32)
    sigma = 1.0 / (1.0 + jnp.exp(-pre_gate))
    active = pre_gate * sigma
    hidden = (active * pre_up).astype(BF)
    gate_back = (back_hidden * pre_up * sigma * (1.0 + pre_gate * (1.0 - sigma))).astype(BF)
    up_back = (back_hidden * active).astype(BF)
    hidden_ref[...] = hidden
    gate_back_ref[...] = gate_back
    up_back_ref[...] = up_back
    route = jnp.sum(hidden.astype(F32) * back_hidden, axis=1, keepdims=True)
    high = route.astype(BF).astype(F32)
    lane = lax.broadcasted_iota(jnp.int32, route_ref.shape, 1)
    route_ref[...] = jnp.where(
        lane == 0, high, jnp.where(lane == 1, route - high, 0.0)
    ).astype(BF)
    copies = []
    for y in range(nblock // 2):
        weight_terms(nblock, y, 1 - core_ref[0], came_ref, hidden, gate_back, up_back, buffer)
        copies.append(pltpu.make_async_copy(buffer.at[y], other_ref.at[y], sems.at[y]))
        copies[-1].start()
    for copy in copies:
        copy.wait()


def weight_terms(nblock, y, core, came_ref, hidden, gate_back, up_back, out_ref):
    width = came_ref.shape[1] // 2
    block = width // nblock
    for which, (base, right) in enumerate(((0, gate_back), (0, up_back), (width, hidden))):
        at = pl.multiple_of(base + (2 * y + core) * block, block)
        out_ref[y, which] = lax.dot_general(
            came_ref[:, pl.ds(at, block)], right, FIRST, preferred_element_type=F32
        ).astype(BF)


def own_body(nblock, core_ref, came_ref, hidden_ref, gate_back_ref, up_back_ref, out_ref):
    for y in range(nblock // 2):
        weight_terms(
            nblock,
            y,
            core_ref[0],
            came_ref,
            hidden_ref[...],
            gate_back_ref[...],
            up_back_ref[...],
            out_ref,
        )


def add_body(own_ref, arrived_ref, out_ref, came, went, in_sems, out_sems):
    steps = own_ref.shape[0]
    reads = [
        pltpu.make_async_copy(arrived_ref.at[y], came.at[y], in_sems.at[y]) for y in range(steps)
    ]
    writes = [
        pltpu.make_async_copy(went.at[y], out_ref.at[y], out_sems.at[y]) for y in range(steps)
    ]
    for read in reads:
        read.start()
    for y in range(steps):
        reads[y].wait()
        went[y] = (own_ref[y].astype(F32) + came[y].astype(F32)).astype(BF)
        writes[y].start()
    for write in writes:
        write.wait()


def final_body(scale, total_ref, gate_ref, up_ref, down_ref):
    block = gate_ref.shape[0]
    gate_ref[...] = total_ref[:block].astype(F32) * scale
    up_ref[...] = total_ref[block : 2 * block].astype(F32) * scale
    down_ref[...] = (total_ref[2 * block :].astype(F32) * scale).T


def sum_body(top, parts_ref, tokens_ref, route_ref):
    width = tokens_ref.shape[1]
    total = parts_ref[0].astype(F32)
    for h in range(1, parts_ref.shape[0]):
        total = total + parts_ref[h].astype(F32)
    tokens_ref[...] = total[:, :width].astype(BF)
    lane = lax.broadcasted_iota(jnp.int32, (top, META), 1)
    row = lax.broadcasted_iota(jnp.int32, (top, META), 0)
    route_ref[...] = lax.dot_general(
        jnp.where(lane == row, 1.0, 0.0).astype(BF),
        total[:, width:].astype(BF),
        LAST,
        preferred_element_type=F32,
    ).astype(BF)


def back_body(gate_back_ref, up_back_ref, route_ref, gate_ref, up_ref, out_ref):
    width = gate_ref.shape[0]
    out = lax.dot_general(gate_back_ref[...], gate_ref[...], LAST, preferred_element_type=F32)
    out = out + lax.dot_general(up_back_ref[...], up_ref[...], LAST, preferred_element_type=F32)
    out_ref[:, :width] = out.astype(BF)
    out_ref[:, width:] = route_ref[...]


def combine_body(top, back_ref, pick_ref, meta_ref, dest_ref, out_ref):
    width = back_ref.shape[1] - META
    pick = pick_ref[...]
    out_ref[:, :width] = jnp.dot(pick, back_ref[:, :width], preferred_element_type=F32).astype(BF)
    lane8 = lax.broadcasted_iota(jnp.int32, (8, META), 1)
    pair = jnp.where(lane8 < 2, 1.0, 0.0).astype(BF)
    route = lax.dot_general(pair, back_ref[:, width:], LAST, preferred_element_type=F32)[0:1]
    mine = jnp.where(pick.astype(F32) > 0.5, route, 0.0)
    meta = meta_ref[...].astype(F32)
    dest = dest_ref[...]
    lane = lax.broadcasted_iota(jnp.int32, (pick.shape[0], META), 1)
    routes = jnp.zeros((pick.shape[0], META), F32)
    for k in range(top):
        value = jnp.sum(
            jnp.where(meta[:, k : k + 1] == dest, mine, 0.0), axis=1, keepdims=True
        )
        routes = jnp.where(lane == k, value / meta[:, top + k : top + k + 1], routes)
    out_ref[:, width:] = routes.astype(BF)


def shards(tokens, expert_ids, route_weights, out_grad, w_gate, w_up, w_down):
    tok, width = tokens.shape
    top = expert_ids.shape[1]
    ff = w_gate.shape[2]
    nx, nh, nl = lax.axis_size("x"), lax.axis_size("zh"), lax.axis_size("zl")
    ny, nc = lax.axis_size("y"), lax.axis_size("core")
    nz = nh * nl
    experts = nx * nz
    cap = min(tok, max(2, 2 * tok * top // experts))
    held = nh * tok
    dests = nx * nl
    per = nh * cap
    slots = dests * per
    nblock = ny * nc
    block = width // nblock

    shift = nl // 2
    groups = [
        [(c * nx + x) * nz + (b * nl + c * shift + l) % nz for x in range(nx) for l in range(nl)]
        for c in range(nc)
        for b in range(nh)
    ]
    core = lax.axis_index("core")
    z = lax.axis_index("zh") * nl + lax.axis_index("zl")
    first = (z - core * shift + nz) % nz // nl * nl + core * shift
    dest = jnp.arange(slots, dtype=jnp.int32) // per
    dest_ids = (dest // nl) * nz + (first + dest % nl) % nz
    dest_ids = dest_ids.astype(F32).reshape(1, slots)
    core_at = core.reshape(1).astype(jnp.int32)

    def forward(a):
        return lax.all_to_all(
            a.reshape(dests, per, -1),
            ("core", "x", "zh", "zl"),
            split_axis=0,
            concat_axis=0,
            tiled=True,
            axis_index_groups=groups,
        ).reshape(slots, -1)

    packed = call(
        functools.partial(pack_body, top),
        jax.ShapeDtypeStruct((tok, 2 * width + META), BF),
        0,
        4 * tok * width,
        ins=[APART] * 4,
        out_specs=VMEM,
        scratch=[
            pltpu.VMEM((top, tok), jnp.int32),
            pltpu.VMEM((top, tok), BF),
            pltpu.SemaphoreType.DMA((4,)),
        ],
        limit=60,
    )(tokens, out_grad, expert_ids.T, route_weights.T)
    gathered = lax.all_gather(packed, "zh", axis=0, tiled=True)

    send, pick, meta = call(
        functools.partial(select_body, tok, cap, top),
        (
            jax.ShapeDtypeStruct((slots, 2 * width), BF),
            jax.ShapeDtypeStruct((held, slots), BF),
            jax.ShapeDtypeStruct((held, META), BF),
        ),
        4 * slots * held * width,
        6 * slots * width,
    )(gathered, dest_ids)
    came = forward(send)

    gate_w, up_w, down_w = w_gate[0], w_up[0], w_down[0]
    small = jax.ShapeDtypeStruct((slots, ff), BF)
    shape = (ny, 3, block, ff)
    terms = jax.ShapeDtypeStruct(shape, BF)
    smem = pl.BlockSpec(memory_space=pltpu.SMEM)
    hidden, gate_back, up_back, route, other = call(
        functools.partial(expert_body, nblock),
        (small, small, small, jax.ShapeDtypeStruct((slots, META), BF), terms),
        9 * slots * ff * width,
        10_000_000,
        ins=[smem] + [VMEM] * 4,
        out_specs=(VMEM,) * 4 + (APART,),
        scratch=[pltpu.VMEM(shape, BF), pltpu.SemaphoreType.DMA((ny,))],
        limit=28,
        exps=slots * ff,
    )(core_at, came, gate_w, up_w, down_w)
    arrived = lax.ppermute(other, "core", [(0, 1), (1, 0)])
    back = call(
        back_body,
        jax.ShapeDtypeStruct((slots, width + META), BF),
        4 * slots * ff * width,
        5_000_000,
    )(gate_back, up_back, route, gate_w, up_w)
    own = call(
        functools.partial(own_body, nblock),
        terms,
        3 * slots * ff * width,
        5_000_000,
        ins=[smem] + [VMEM] * 4,
    )(core_at, came, hidden, gate_back, up_back)
    pair = call(
        add_body,
        terms,
        0,
        7_000_000,
        ins=[VMEM, APART],
        out_specs=APART,
        scratch=[
            pltpu.VMEM(shape, BF),
            pltpu.VMEM(shape, BF),
            pltpu.SemaphoreType.DMA((ny,)),
            pltpu.SemaphoreType.DMA((ny,)),
        ],
    )(own, arrived)
    pair, back = lax.optimization_barrier((pair, back))
    total = lax.psum_scatter(
        pair.reshape(ny * 3 * block, ff), "y", scatter_dimension=0, tiled=True
    )
    grads = call(
        functools.partial(final_body, 1.0 / nblock),
        (
            jax.ShapeDtypeStruct((block, ff), F32),
            jax.ShapeDtypeStruct((block, ff), F32),
            jax.ShapeDtypeStruct((ff, block), F32),
        ),
        0,
        9 * block * ff,
    )(total)

    back = forward(back)
    outgoing = call(
        functools.partial(combine_body, top),
        jax.ShapeDtypeStruct((held, width + META), BF),
        2 * slots * held * width,
        2_000_000,
    )(back, pick, meta, dest_ids)
    parts = lax.all_to_all(
        outgoing.reshape(nh, tok, -1), "zh", split_axis=0, concat_axis=0, tiled=True
    )
    grad_tokens, grad_route = call(
        functools.partial(sum_body, top),
        (jax.ShapeDtypeStruct((tok, width), BF), jax.ShapeDtypeStruct((top, tok), BF)),
        0,
        10 * tok * width,
    )(parts)
    return (grad_tokens, grad_route.T) + tuple(g[None] for g in grads)


def solution(mesh):
    groups, experts = mesh.devices.shape
    n = round(experts ** (1 / 3))
    fine = Mesh(
        mesh.devices.reshape(groups // 2, 2, n, n, n), ("y", "core", "x", "zh", "zl")
    )
    dp = ("y", "core")
    ex = ("x", "zh", "zl")
    rows = P(dp + ex, None)
    return jax.shard_map(
        shards,
        mesh=fine,
        in_specs=(rows, rows, rows, rows) + (P(ex, None, None),) * 3,
        out_specs=(rows, rows, P(ex, dp, None), P(ex, dp, None), P(ex, None, dp)),
        check_vma=False,
    )
```

```python
import functools

import jax
import jax.numpy as jnp
from jax import lax
from jax.experimental import pallas as pl
from jax.experimental.pallas import tpu as pltpu
from jax.sharding import Mesh
from jax.sharding import PartitionSpec as P

BF = jnp.bfloat16
F32 = jnp.float32
META = 128
VMEM = pl.BlockSpec(memory_space=pltpu.VMEM)
APART = pl.BlockSpec(memory_space=pltpu.HBM)
FIRST = (((0,), (0,)), ((), ()))
LAST = (((1,), (1,)), ((), ()))


def call(body, outs, flops, moved, ins=None, scratch=(), limit=16, exps=0, out_specs=None):
    extra = {} if ins is None else {"in_specs": ins}
    if out_specs is not None:
        extra["out_specs"] = out_specs
    return pl.pallas_call(
        body,
        out_shape=outs,
        scratch_shapes=scratch,
        compiler_params=pltpu.CompilerParams(vmem_limit_bytes=limit * 1024 * 1024),
        cost_estimate=pl.CostEstimate(flops=flops, bytes_accessed=moved, transcendentals=exps),
        **extra,
    )


def pack_body(top, tokens_ref, cots_ref, ids_ref, weights_ref, out_ref, ids_here, weights_here, sems):
    width = tokens_ref.shape[1]
    copies = [
        pltpu.make_async_copy(source, target, sems.at[n])
        for n, (source, target) in enumerate(
            (
                (ids_ref, ids_here),
                (weights_ref, weights_here),
                (tokens_ref, out_ref.at[:, pl.ds(0, width)]),
                (cots_ref, out_ref.at[:, pl.ds(width, width)]),
            )
        )
    ]
    for copy in copies:
        copy.start()
    lane = lax.broadcasted_iota(jnp.int32, (top, META), 1)
    row = lax.broadcasted_iota(jnp.int32, (top, META), 0)
    copies[0].wait()
    copies[1].wait()
    meta = lax.dot_general(
        ids_here[...].astype(F32).astype(BF),
        jnp.where(lane == row, 1.0, 0.0).astype(BF),
        FIRST,
        preferred_element_type=F32,
    ) + lax.dot_general(
        weights_here[...].astype(F32).astype(BF),
        jnp.where(lane == row + top, 1.0, 0.0).astype(BF),
        FIRST,
        preferred_element_type=F32,
    )
    out_ref[:, 2 * width :] = meta.astype(BF)
    copies[2].wait()
    copies[3].wait()


def select_body(tok, cap, top, held_ref, dest_ref, send_ref, pick_ref, meta_ref):
    held = held_ref.shape[0]
    slots, width = send_ref.shape[0], send_ref.shape[1] // 2
    meta_ref[...] = held_ref[:, 2 * width :]
    meta = held_ref[:, 2 * width :].astype(F32)
    dest = dest_ref[...]
    match = jnp.zeros((held, slots), F32)
    weight = jnp.zeros((held, slots), F32)
    for k in range(top):
        same = meta[:, k : k + 1] == dest
        match = jnp.where(same, 1.0, match)
        weight = jnp.where(same, meta[:, top + k : top + k + 1], weight)
    row = lax.broadcasted_iota(jnp.int32, (held, held), 0)
    col = lax.broadcasted_iota(jnp.int32, (held, held), 1)
    earlier = jnp.where((col < row) & (col // tok == row // tok), 1.0, 0.0).astype(BF)
    position = jnp.dot(earlier, match.astype(BF), preferred_element_type=F32).astype(jnp.int32)
    token = lax.broadcasted_iota(jnp.int32, (held, slots), 0)
    slot = lax.broadcasted_iota(jnp.int32, (held, slots), 1) % (held // tok * cap)
    pick = (match > 0.5) & (position + token // tok * cap == slot) & (position < cap)
    flat = jnp.where(pick, 1.0, 0.0).astype(BF)
    scaled = jnp.where(pick, weight, 0.0).astype(BF)
    pick_ref[...] = flat
    for half, chosen in ((0, flat), (1, scaled)):
        send_ref[:, half * width : (half + 1) * width] = lax.dot_general(
            chosen,
            held_ref[:, half * width : (half + 1) * width],
            FIRST,
            preferred_element_type=F32,
        ).astype(BF)


def expert_body(
    nblock,
    core_ref,
    came_ref,
    gate_ref,
    up_ref,
    down_ref,
    hidden_ref,
    gate_back_ref,
    up_back_ref,
    route_ref,
    other_ref,
    buffer,
    sems,
):
    width = came_ref.shape[1] // 2
    inputs, scaled = came_ref[:, :width], came_ref[:, width:]
    pre_gate = jnp.dot(inputs, gate_ref[...], preferred_element_type=F32)
    pre_up = jnp.dot(inputs, up_ref[...], preferred_element_type=F32)
    back_hidden = lax.dot_general(scaled, down_ref[...], LAST, preferred_element_type=F32)
    sigma = 1.0 / (1.0 + jnp.exp(-pre_gate))
    active = pre_gate * sigma
    hidden = (active * pre_up).astype(BF)
    gate_back = (back_hidden * pre_up * sigma * (1.0 + pre_gate * (1.0 - sigma))).astype(BF)
    up_back = (back_hidden * active).astype(BF)
    hidden_ref[...] = hidden
    gate_back_ref[...] = gate_back
    up_back_ref[...] = up_back
    route = jnp.sum(hidden.astype(F32) * back_hidden, axis=1, keepdims=True)
    high = route.astype(BF).astype(F32)
    lane = lax.broadcasted_iota(jnp.int32, route_ref.shape, 1)
    route_ref[...] = jnp.where(
        lane == 0, high, jnp.where(lane == 1, route - high, 0.0)
    ).astype(BF)
    copies = []
    for y in range(nblock // 2):
        weight_terms(nblock, y, 1 - core_ref[0], came_ref, hidden, gate_back, up_back, buffer)
        copies.append(pltpu.make_async_copy(buffer.at[y], other_ref.at[y], sems.at[y]))
        copies[-1].start()
    for copy in copies:
        copy.wait()


def weight_terms(nblock, y, core, came_ref, hidden, gate_back, up_back, out_ref):
    width = came_ref.shape[1] // 2
    block = width // nblock
    for which, (base, right) in enumerate(((0, gate_back), (0, up_back), (width, hidden))):
        at = pl.multiple_of(base + (2 * y + core) * block, block)
        out_ref[y, which] = lax.dot_general(
            came_ref[:, pl.ds(at, block)], right, FIRST, preferred_element_type=F32
        ).astype(BF)


def own_body(nblock, core_ref, came_ref, hidden_ref, gate_back_ref, up_back_ref, out_ref):
    for y in range(nblock // 2):
        weight_terms(
            nblock,
            y,
            core_ref[0],
            came_ref,
            hidden_ref[...],
            gate_back_ref[...],
            up_back_ref[...],
            out_ref,
        )


def add_body(own_ref, arrived_ref, out_ref, went, sems):
    writes = []
    for y in range(own_ref.shape[0]):
        went[y] = (own_ref[y].astype(F32) + arrived_ref[y].astype(F32)).astype(BF)
        writes.append(pltpu.make_async_copy(went.at[y], out_ref.at[y], sems.at[y]))
        writes[-1].start()
    for write in writes:
        write.wait()


def final_body(scale, total_ref, gate_ref, up_ref, down_ref):
    block = gate_ref.shape[0]
    gate_ref[...] = total_ref[:block].astype(F32) * scale
    up_ref[...] = total_ref[block : 2 * block].astype(F32) * scale
    down_ref[...] = (total_ref[2 * block :].astype(F32) * scale).T


def sum_body(top, parts_ref, tokens_ref, route_ref):
    width = tokens_ref.shape[1]
    total = parts_ref[0].astype(F32)
    for h in range(1, parts_ref.shape[0]):
        total = total + parts_ref[h].astype(F32)
    tokens_ref[...] = total[:, :width].astype(BF)
    lane = lax.broadcasted_iota(jnp.int32, (top, META), 1)
    row = lax.broadcasted_iota(jnp.int32, (top, META), 0)
    route_ref[...] = lax.dot_general(
        jnp.where(lane == row, 1.0, 0.0).astype(BF),
        total[:, width:].astype(BF),
        LAST,
        preferred_element_type=F32,
    ).astype(BF)


def back_body(gate_back_ref, up_back_ref, route_ref, gate_ref, up_ref, out_ref):
    width = gate_ref.shape[0]
    out = lax.dot_general(gate_back_ref[...], gate_ref[...], LAST, preferred_element_type=F32)
    out = out + lax.dot_general(up_back_ref[...], up_ref[...], LAST, preferred_element_type=F32)
    out_ref[:, :width] = out.astype(BF)
    out_ref[:, width:] = route_ref[...]


def combine_body(top, back_ref, pick_ref, meta_ref, dest_ref, out_ref):
    width = back_ref.shape[1] - META
    pick = pick_ref[...]
    out_ref[:, :width] = jnp.dot(pick, back_ref[:, :width], preferred_element_type=F32).astype(BF)
    lane8 = lax.broadcasted_iota(jnp.int32, (8, META), 1)
    pair = jnp.where(lane8 < 2, 1.0, 0.0).astype(BF)
    route = lax.dot_general(pair, back_ref[:, width:], LAST, preferred_element_type=F32)[0:1]
    mine = jnp.where(pick.astype(F32) > 0.5, route, 0.0)
    meta = meta_ref[...].astype(F32)
    dest = dest_ref[...]
    lane = lax.broadcasted_iota(jnp.int32, (pick.shape[0], META), 1)
    routes = jnp.zeros((pick.shape[0], META), F32)
    for k in range(top):
        value = jnp.sum(
            jnp.where(meta[:, k : k + 1] == dest, mine, 0.0), axis=1, keepdims=True
        )
        routes = jnp.where(lane == k, value / meta[:, top + k : top + k + 1], routes)
    out_ref[:, width:] = routes.astype(BF)


def shards(tokens, expert_ids, route_weights, out_grad, w_gate, w_up, w_down):
    tok, width = tokens.shape
    top = expert_ids.shape[1]
    ff = w_gate.shape[2]
    nx, nh, nl = lax.axis_size("x"), lax.axis_size("zh"), lax.axis_size("zl")
    ny, nc = lax.axis_size("y"), lax.axis_size("core")
    nz = nh * nl
    experts = nx * nz
    cap = min(tok, max(2, 2 * tok * top // experts))
    held = nh * tok
    dests = nx * nl
    per = nh * cap
    slots = dests * per
    nblock = ny * nc
    block = width // nblock

    shift = nl // 2
    groups = [
        [(c * nx + x) * nz + (b * nl + c * shift + l) % nz for x in range(nx) for l in range(nl)]
        for c in range(nc)
        for b in range(nh)
    ]
    core = lax.axis_index("core")
    z = lax.axis_index("zh") * nl + lax.axis_index("zl")
    first = (z - core * shift + nz) % nz // nl * nl + core * shift
    dest = jnp.arange(slots, dtype=jnp.int32) // per
    dest_ids = (dest // nl) * nz + (first + dest % nl) % nz
    dest_ids = dest_ids.astype(F32).reshape(1, slots)
    core_at = core.reshape(1).astype(jnp.int32)

    def forward(a):
        return lax.all_to_all(
            a.reshape(dests, per, -1),
            ("core", "x", "zh", "zl"),
            split_axis=0,
            concat_axis=0,
            tiled=True,
            axis_index_groups=groups,
        ).reshape(slots, -1)

    packed = call(
        functools.partial(pack_body, top),
        jax.ShapeDtypeStruct((tok, 2 * width + META), BF),
        0,
        4 * tok * width,
        ins=[APART] * 4,
        out_specs=VMEM,
        scratch=[
            pltpu.VMEM((top, tok), jnp.int32),
            pltpu.VMEM((top, tok), BF),
            pltpu.SemaphoreType.DMA((4,)),
        ],
        limit=60,
    )(tokens, out_grad, expert_ids.T, route_weights.T)
    gathered = lax.all_gather(packed, "zh", axis=0, tiled=True)

    send, pick, meta = call(
        functools.partial(select_body, tok, cap, top),
        (
            jax.ShapeDtypeStruct((slots, 2 * width), BF),
            jax.ShapeDtypeStruct((held, slots), BF),
            jax.ShapeDtypeStruct((held, META), BF),
        ),
        4 * slots * held * width,
        6 * slots * width,
    )(gathered, dest_ids)
    came = forward(send)

    gate_w, up_w, down_w = w_gate[0], w_up[0], w_down[0]
    small = jax.ShapeDtypeStruct((slots, ff), BF)
    shape = (ny, 3, block, ff)
    terms = jax.ShapeDtypeStruct(shape, BF)
    smem = pl.BlockSpec(memory_space=pltpu.SMEM)
    hidden, gate_back, up_back, route, other = call(
        functools.partial(expert_body, nblock),
        (small, small, small, jax.ShapeDtypeStruct((slots, META), BF), terms),
        9 * slots * ff * width,
        10_000_000,
        ins=[smem] + [VMEM] * 4,
        out_specs=(VMEM,) * 4 + (APART,),
        scratch=[pltpu.VMEM(shape, BF), pltpu.SemaphoreType.DMA((ny,))],
        limit=28,
        exps=slots * ff,
    )(core_at, came, gate_w, up_w, down_w)
    arrived = lax.ppermute(other, "core", [(0, 1), (1, 0)])
    back = call(
        back_body,
        jax.ShapeDtypeStruct((slots, width + META), BF),
        4 * slots * ff * width,
        5_000_000,
    )(gate_back, up_back, route, gate_w, up_w)
    own = call(
        functools.partial(own_body, nblock),
        terms,
        3 * slots * ff * width,
        5_000_000,
        ins=[smem] + [VMEM] * 4,
    )(core_at, came, hidden, gate_back, up_back)
    pair = call(
        add_body,
        terms,
        0,
        7_000_000,
        ins=[VMEM, VMEM],
        out_specs=APART,
        scratch=[pltpu.VMEM(shape, BF), pltpu.SemaphoreType.DMA((ny,))],
    )(own, arrived)
    pair, back = lax.optimization_barrier((pair, back))
    total = lax.psum_scatter(
        pair.reshape(ny * 3 * block, ff), "y", scatter_dimension=0, tiled=True
    )
    grads = call(
        functools.partial(final_body, 1.0 / nblock),
        (
            jax.ShapeDtypeStruct((block, ff), F32),
            jax.ShapeDtypeStruct((block, ff), F32),
            jax.ShapeDtypeStruct((ff, block), F32),
        ),
        0,
        9 * block * ff,
    )(total)

    def way_back(back, pick, meta, dest_ids):
        back = forward(back)
        outgoing = call(
            functools.partial(combine_body, top),
            jax.ShapeDtypeStruct((held, width + META), BF),
            2 * slots * held * width,
            2_000_000,
        )(back, pick, meta, dest_ids)
        parts = lax.all_to_all(
            outgoing.reshape(nh, tok, -1), "zh", split_axis=0, concat_axis=0, tiled=True
        )
        grad_tokens, grad_route = call(
            functools.partial(sum_body, top),
            (jax.ShapeDtypeStruct((tok, width), BF), jax.ShapeDtypeStruct((top, tok), BF)),
            0,
            10 * tok * width,
        )(parts)
        return grad_tokens, grad_route

    grad_tokens, grad_route = lax.cond(
        route_weights[0, 0] > 0, way_back, way_back, back, pick, meta, dest_ids
    )
    return (grad_tokens, grad_route.T) + tuple(g[None] for g in grads)


def solution(mesh):
    groups, experts = mesh.devices.shape
    n = round(experts ** (1 / 3))
    fine = Mesh(
        mesh.devices.reshape(groups // 2, 2, n, n, n), ("y", "core", "x", "zh", "zl")
    )
    dp = ("y", "core")
    ex = ("x", "zh", "zl")
    rows = P(dp + ex, None)
    return jax.shard_map(
        shards,
        mesh=fine,
        in_specs=(rows, rows, rows, rows) + (P(ex, None, None),) * 3,
        out_specs=(rows, rows, P(ex, dp, None), P(ex, dp, None), P(ex, None, dp)),
        check_vma=False,
    )
```

```python
import functools

import jax
import jax.numpy as jnp
from jax import lax
from jax.experimental import pallas as pl
from jax.experimental.pallas import tpu as pltpu
from jax.sharding import Mesh
from jax.sharding import PartitionSpec as P

BF = jnp.bfloat16
F32 = jnp.float32
META = 128
VMEM = pl.BlockSpec(memory_space=pltpu.VMEM)
APART = pl.BlockSpec(memory_space=pltpu.HBM)
FIRST = (((0,), (0,)), ((), ()))
LAST = (((1,), (1,)), ((), ()))


def call(body, outs, flops, moved, ins=None, scratch=(), limit=16, exps=0, out_specs=None):
    extra = {} if ins is None else {"in_specs": ins}
    if out_specs is not None:
        extra["out_specs"] = out_specs
    return pl.pallas_call(
        body,
        out_shape=outs,
        scratch_shapes=scratch,
        compiler_params=pltpu.CompilerParams(vmem_limit_bytes=limit * 1024 * 1024),
        cost_estimate=pl.CostEstimate(flops=flops, bytes_accessed=moved, transcendentals=exps),
        **extra,
    )


def pack_body(top, tokens_ref, cots_ref, ids_ref, weights_ref, out_ref, ids_here, weights_here, sems):
    width = tokens_ref.shape[1]
    copies = [
        pltpu.make_async_copy(source, target, sems.at[n])
        for n, (source, target) in enumerate(
            (
                (ids_ref, ids_here),
                (weights_ref, weights_here),
                (tokens_ref, out_ref.at[:, pl.ds(0, width)]),
                (cots_ref, out_ref.at[:, pl.ds(width, width)]),
            )
        )
    ]
    for copy in copies:
        copy.start()
    lane = lax.broadcasted_iota(jnp.int32, (top, META), 1)
    row = lax.broadcasted_iota(jnp.int32, (top, META), 0)
    copies[0].wait()
    copies[1].wait()
    meta = lax.dot_general(
        ids_here[...].astype(F32).astype(BF),
        jnp.where(lane == row, 1.0, 0.0).astype(BF),
        FIRST,
        preferred_element_type=F32,
    ) + lax.dot_general(
        weights_here[...].astype(F32).astype(BF),
        jnp.where(lane == row + top, 1.0, 0.0).astype(BF),
        FIRST,
        preferred_element_type=F32,
    )
    out_ref[:, 2 * width :] = meta.astype(BF)
    copies[2].wait()
    copies[3].wait()


def select_body(tok, cap, top, held_ref, dest_ref, send_ref, pick_ref, meta_ref):
    held = held_ref.shape[0]
    slots, width = send_ref.shape[0], send_ref.shape[1] // 2
    meta_ref[...] = held_ref[:, 2 * width :]
    meta = held_ref[:, 2 * width :].astype(F32)
    dest = dest_ref[...]
    match = jnp.zeros((held, slots), F32)
    weight = jnp.zeros((held, slots), F32)
    for k in range(top):
        same = meta[:, k : k + 1] == dest
        match = jnp.where(same, 1.0, match)
        weight = jnp.where(same, meta[:, top + k : top + k + 1], weight)
    row = lax.broadcasted_iota(jnp.int32, (held, held), 0)
    col = lax.broadcasted_iota(jnp.int32, (held, held), 1)
    earlier = jnp.where((col < row) & (col // tok == row // tok), 1.0, 0.0).astype(BF)
    position = jnp.dot(earlier, match.astype(BF), preferred_element_type=F32).astype(jnp.int32)
    token = lax.broadcasted_iota(jnp.int32, (held, slots), 0)
    slot = lax.broadcasted_iota(jnp.int32, (held, slots), 1) % (held // tok * cap)
    pick = (match > 0.5) & (position + token // tok * cap == slot) & (position < cap)
    flat = jnp.where(pick, 1.0, 0.0).astype(BF)
    scaled = jnp.where(pick, weight, 0.0).astype(BF)
    pick_ref[...] = flat
    for half, chosen in ((0, flat), (1, scaled)):
        send_ref[:, half * width : (half + 1) * width] = lax.dot_general(
            chosen,
            held_ref[:, half * width : (half + 1) * width],
            FIRST,
            preferred_element_type=F32,
        ).astype(BF)


def expert_body(
    nblock,
    core_ref,
    came_ref,
    gate_ref,
    up_ref,
    down_ref,
    hidden_ref,
    gate_back_ref,
    up_back_ref,
    route_ref,
    other_ref,
):
    width = came_ref.shape[1] // 2
    inputs, scaled = came_ref[:, :width], came_ref[:, width:]
    pre_gate = jnp.dot(inputs, gate_ref[...], preferred_element_type=F32)
    pre_up = jnp.dot(inputs, up_ref[...], preferred_element_type=F32)
    back_hidden = lax.dot_general(scaled, down_ref[...], LAST, preferred_element_type=F32)
    sigma = 1.0 / (1.0 + jnp.exp(-pre_gate))
    active = pre_gate * sigma
    hidden = (active * pre_up).astype(BF)
    gate_back = (back_hidden * pre_up * sigma * (1.0 + pre_gate * (1.0 - sigma))).astype(BF)
    up_back = (back_hidden * active).astype(BF)
    hidden_ref[...] = hidden
    gate_back_ref[...] = gate_back
    up_back_ref[...] = up_back
    route = jnp.sum(hidden.astype(F32) * back_hidden, axis=1, keepdims=True)
    high = route.astype(BF).astype(F32)
    lane = lax.broadcasted_iota(jnp.int32, route_ref.shape, 1)
    route_ref[...] = jnp.where(
        lane == 0, high, jnp.where(lane == 1, route - high, 0.0)
    ).astype(BF)
    for y in range(nblock // 2):
        weight_terms(nblock, y, 1 - core_ref[0], came_ref, hidden, gate_back, up_back, other_ref)


def weight_terms(nblock, y, core, came_ref, hidden, gate_back, up_back, out_ref):
    width = came_ref.shape[1] // 2
    block = width // nblock
    for which, (base, right) in enumerate(((0, gate_back), (0, up_back), (width, hidden))):
        at = pl.multiple_of(base + (2 * y + core) * block, block)
        out_ref[y, which] = lax.dot_general(
            came_ref[:, pl.ds(at, block)], right, FIRST, preferred_element_type=F32
        ).astype(BF)


def own_body(nblock, core_ref, came_ref, hidden_ref, gate_back_ref, up_back_ref, out_ref):
    for y in range(nblock // 2):
        weight_terms(
            nblock,
            y,
            core_ref[0],
            came_ref,
            hidden_ref[...],
            gate_back_ref[...],
            up_back_ref[...],
            out_ref,
        )


def add_body(own_ref, arrived_ref, out_ref, came, went, in_sems, out_sems):
    steps = own_ref.shape[0]
    reads = [
        pltpu.make_async_copy(arrived_ref.at[y], came.at[y], in_sems.at[y]) for y in range(steps)
    ]
    writes = [
        pltpu.make_async_copy(went.at[y], out_ref.at[y], out_sems.at[y]) for y in range(steps)
    ]
    for read in reads:
        read.start()
    for y in range(steps):
        reads[y].wait()
        went[y] = (own_ref[y].astype(F32) + came[y].astype(F32)).astype(BF)
        writes[y].start()
    for write in writes:
        write.wait()


def final_body(scale, total_ref, gate_ref, up_ref, down_ref):
    block = gate_ref.shape[0]
    gate_ref[...] = total_ref[:block].astype(F32) * scale
    up_ref[...] = total_ref[block : 2 * block].astype(F32) * scale
    down_ref[...] = (total_ref[2 * block :].astype(F32) * scale).T


def sum_body(top, parts_ref, tokens_ref, route_ref):
    width = tokens_ref.shape[1]
    total = parts_ref[0].astype(F32)
    for h in range(1, parts_ref.shape[0]):
        total = total + parts_ref[h].astype(F32)
    tokens_ref[...] = total[:, :width].astype(BF)
    lane = lax.broadcasted_iota(jnp.int32, (top, META), 1)
    row = lax.broadcasted_iota(jnp.int32, (top, META), 0)
    route_ref[...] = lax.dot_general(
        jnp.where(lane == row, 1.0, 0.0).astype(BF),
        total[:, width:].astype(BF),
        LAST,
        preferred_element_type=F32,
    ).astype(BF)


def back_body(gate_back_ref, up_back_ref, route_ref, gate_ref, up_ref, out_ref):
    width = gate_ref.shape[0]
    out = lax.dot_general(gate_back_ref[...], gate_ref[...], LAST, preferred_element_type=F32)
    out = out + lax.dot_general(up_back_ref[...], up_ref[...], LAST, preferred_element_type=F32)
    out_ref[:, :width] = out.astype(BF)
    out_ref[:, width:] = route_ref[...]


def combine_body(top, back_ref, pick_ref, meta_ref, dest_ref, out_ref):
    width = back_ref.shape[1] - META
    pick = pick_ref[...]
    out_ref[:, :width] = jnp.dot(pick, back_ref[:, :width], preferred_element_type=F32).astype(BF)
    lane8 = lax.broadcasted_iota(jnp.int32, (8, META), 1)
    pair = jnp.where(lane8 < 2, 1.0, 0.0).astype(BF)
    route = lax.dot_general(pair, back_ref[:, width:], LAST, preferred_element_type=F32)[0:1]
    mine = jnp.where(pick.astype(F32) > 0.5, route, 0.0)
    meta = meta_ref[...].astype(F32)
    dest = dest_ref[...]
    lane = lax.broadcasted_iota(jnp.int32, (pick.shape[0], META), 1)
    routes = jnp.zeros((pick.shape[0], META), F32)
    for k in range(top):
        value = jnp.sum(
            jnp.where(meta[:, k : k + 1] == dest, mine, 0.0), axis=1, keepdims=True
        )
        routes = jnp.where(lane == k, value / meta[:, top + k : top + k + 1], routes)
    out_ref[:, width:] = routes.astype(BF)


def shards(tokens, expert_ids, route_weights, out_grad, w_gate, w_up, w_down):
    tok, width = tokens.shape
    top = expert_ids.shape[1]
    ff = w_gate.shape[2]
    nx, nh, nl = lax.axis_size("x"), lax.axis_size("zh"), lax.axis_size("zl")
    ny, nc = lax.axis_size("y"), lax.axis_size("core")
    nz = nh * nl
    experts = nx * nz
    cap = min(tok, max(2, 2 * tok * top // experts))
    held = nh * tok
    dests = nx * nl
    per = nh * cap
    slots = dests * per
    nblock = ny * nc
    block = width // nblock

    shift = nl // 2
    groups = [
        [(c * nx + x) * nz + (b * nl + c * shift + l) % nz for x in range(nx) for l in range(nl)]
        for c in range(nc)
        for b in range(nh)
    ]
    core = lax.axis_index("core")
    z = lax.axis_index("zh") * nl + lax.axis_index("zl")
    first = (z - core * shift + nz) % nz // nl * nl + core * shift
    dest = jnp.arange(slots, dtype=jnp.int32) // per
    dest_ids = (dest // nl) * nz + (first + dest % nl) % nz
    dest_ids = dest_ids.astype(F32).reshape(1, slots)
    core_at = core.reshape(1).astype(jnp.int32)

    def forward(a):
        return lax.all_to_all(
            a.reshape(dests, per, -1),
            ("core", "x", "zh", "zl"),
            split_axis=0,
            concat_axis=0,
            tiled=True,
            axis_index_groups=groups,
        ).reshape(slots, -1)

    packed = call(
        functools.partial(pack_body, top),
        jax.ShapeDtypeStruct((tok, 2 * width + META), BF),
        0,
        4 * tok * width,
        ins=[APART] * 4,
        out_specs=VMEM,
        scratch=[
            pltpu.VMEM((top, tok), jnp.int32),
            pltpu.VMEM((top, tok), BF),
            pltpu.SemaphoreType.DMA((4,)),
        ],
        limit=60,
    )(tokens, out_grad, expert_ids.T, route_weights.T)
    gathered = lax.all_gather(packed, "zh", axis=0, tiled=True)

    send, pick, meta = call(
        functools.partial(select_body, tok, cap, top),
        (
            jax.ShapeDtypeStruct((slots, 2 * width), BF),
            jax.ShapeDtypeStruct((held, slots), BF),
            jax.ShapeDtypeStruct((held, META), BF),
        ),
        4 * slots * held * width,
        6 * slots * width,
    )(gathered, dest_ids)
    came = forward(send)

    gate_w, up_w, down_w = w_gate[0], w_up[0], w_down[0]
    small = jax.ShapeDtypeStruct((slots, ff), BF)
    shape = (ny, 3, block, ff)
    terms = jax.ShapeDtypeStruct(shape, BF)
    smem = pl.BlockSpec(memory_space=pltpu.SMEM)
    hidden, gate_back, up_back, route, other = call(
        functools.partial(expert_body, nblock),
        (small, small, small, jax.ShapeDtypeStruct((slots, META), BF), terms),
        9 * slots * ff * width,
        10_000_000,
        ins=[smem] + [VMEM] * 4,
        limit=28,
        exps=slots * ff,
    )(core_at, came, gate_w, up_w, down_w)
    arrived = lax.ppermute(other, "core", [(0, 1), (1, 0)])
    back = call(
        back_body,
        jax.ShapeDtypeStruct((slots, width + META), BF),
        4 * slots * ff * width,
        5_000_000,
    )(gate_back, up_back, route, gate_w, up_w)
    own = call(
        functools.partial(own_body, nblock),
        terms,
        3 * slots * ff * width,
        5_000_000,
        ins=[smem] + [VMEM] * 4,
    )(core_at, came, hidden, gate_back, up_back)
    own, back = lax.optimization_barrier((own, back))
    pair = call(
        add_body,
        terms,
        0,
        7_000_000,
        ins=[VMEM, APART],
        out_specs=APART,
        scratch=[
            pltpu.VMEM(shape, BF),
            pltpu.VMEM(shape, BF),
            pltpu.SemaphoreType.DMA((ny,)),
            pltpu.SemaphoreType.DMA((ny,)),
        ],
    )(own, arrived)
    total = lax.psum_scatter(
        pair.reshape(ny * 3 * block, ff), "y", scatter_dimension=0, tiled=True
    )
    grads = call(
        functools.partial(final_body, 1.0 / nblock),
        (
            jax.ShapeDtypeStruct((block, ff), F32),
            jax.ShapeDtypeStruct((block, ff), F32),
            jax.ShapeDtypeStruct((ff, block), F32),
        ),
        0,
        9 * block * ff,
        limit=60,
    )(total)

    back = forward(back)
    outgoing = call(
        functools.partial(combine_body, top),
        jax.ShapeDtypeStruct((held, width + META), BF),
        2 * slots * held * width,
        2_000_000,
    )(back, pick, meta, dest_ids)
    parts = lax.all_to_all(
        outgoing.reshape(nh, tok, -1), "zh", split_axis=0, concat_axis=0, tiled=True
    )
    grad_tokens, grad_route = call(
        functools.partial(sum_body, top),
        (jax.ShapeDtypeStruct((tok, width), BF), jax.ShapeDtypeStruct((top, tok), BF)),
        0,
        10 * tok * width,
    )(parts)
    return (grad_tokens, grad_route.T) + tuple(g[None] for g in grads)


def solution(mesh):
    groups, experts = mesh.devices.shape
    n = round(experts ** (1 / 3))
    fine = Mesh(
        mesh.devices.reshape(groups // 2, 2, n, n, n), ("y", "core", "x", "zh", "zl")
    )
    dp = ("y", "core")
    ex = ("x", "zh", "zl")
    rows = P(dp + ex, None)
    return jax.shard_map(
        shards,
        mesh=fine,
        in_specs=(rows, rows, rows, rows) + (P(ex, None, None),) * 3,
        out_specs=(rows, rows, P(ex, dp, None), P(ex, dp, None), P(ex, None, dp)),
        check_vma=False,
    )
```

```python
import functools

import jax
import jax.numpy as jnp
from jax import lax
from jax.experimental import pallas as pl
from jax.experimental.pallas import tpu as pltpu
from jax.sharding import Mesh
from jax.sharding import PartitionSpec as P

BF = jnp.bfloat16
F32 = jnp.float32
META = 128
VMEM = pl.BlockSpec(memory_space=pltpu.VMEM)
APART = pl.BlockSpec(memory_space=pltpu.HBM)
FIRST = (((0,), (0,)), ((), ()))
LAST = (((1,), (1,)), ((), ()))


def call(body, outs, flops, moved, ins=None, scratch=(), limit=16, exps=0, out_specs=None):
    extra = {} if ins is None else {"in_specs": ins}
    if out_specs is not None:
        extra["out_specs"] = out_specs
    return pl.pallas_call(
        body,
        out_shape=outs,
        scratch_shapes=scratch,
        compiler_params=pltpu.CompilerParams(vmem_limit_bytes=limit * 1024 * 1024),
        cost_estimate=pl.CostEstimate(flops=flops, bytes_accessed=moved, transcendentals=exps),
        **extra,
    )


def pack_body(top, tokens_ref, cots_ref, ids_ref, weights_ref, out_ref, ids_here, weights_here, meta_here, sems):
    width = tokens_ref.shape[1]
    copies = [
        pltpu.make_async_copy(source, target, sems.at[n])
        for n, (source, target) in enumerate(
            (
                (ids_ref, ids_here),
                (weights_ref, weights_here),
                (tokens_ref, out_ref.at[:, pl.ds(0, width)]),
                (cots_ref, out_ref.at[:, pl.ds(width, width)]),
            )
        )
    ]
    for copy in copies:
        copy.start()
    lane = lax.broadcasted_iota(jnp.int32, (top, META), 1)
    row = lax.broadcasted_iota(jnp.int32, (top, META), 0)
    copies[0].wait()
    copies[1].wait()
    meta = lax.dot_general(
        ids_here[...].astype(F32).astype(BF),
        jnp.where(lane == row, 1.0, 0.0).astype(BF),
        FIRST,
        preferred_element_type=F32,
    ) + lax.dot_general(
        weights_here[...].astype(F32).astype(BF),
        jnp.where(lane == row + top, 1.0, 0.0).astype(BF),
        FIRST,
        preferred_element_type=F32,
    )
    meta_here[...] = meta.astype(BF)
    last = pltpu.make_async_copy(
        meta_here, out_ref.at[:, pl.ds(2 * width, META)], sems.at[4]
    )
    last.start()
    copies[2].wait()
    copies[3].wait()
    last.wait()


def select_body(tok, cap, top, held_ref, dest_ref, send_ref, pick_ref, meta_ref):
    held = held_ref.shape[0]
    slots, width = send_ref.shape[0], send_ref.shape[1] // 2
    meta_ref[...] = held_ref[:, 2 * width :]
    meta = held_ref[:, 2 * width :].astype(F32)
    dest = dest_ref[...]
    match = jnp.zeros((held, slots), F32)
    weight = jnp.zeros((held, slots), F32)
    for k in range(top):
        same = meta[:, k : k + 1] == dest
        match = jnp.where(same, 1.0, match)
        weight = jnp.where(same, meta[:, top + k : top + k + 1], weight)
    row = lax.broadcasted_iota(jnp.int32, (held, held), 0)
    col = lax.broadcasted_iota(jnp.int32, (held, held), 1)
    earlier = jnp.where((col < row) & (col // tok == row // tok), 1.0, 0.0).astype(BF)
    position = jnp.dot(earlier, match.astype(BF), preferred_element_type=F32).astype(jnp.int32)
    token = lax.broadcasted_iota(jnp.int32, (held, slots), 0)
    slot = lax.broadcasted_iota(jnp.int32, (held, slots), 1) % (held // tok * cap)
    pick = (match > 0.5) & (position + token // tok * cap == slot) & (position < cap)
    flat = jnp.where(pick, 1.0, 0.0).astype(BF)
    scaled = jnp.where(pick, weight, 0.0).astype(BF)
    pick_ref[...] = flat
    for half, chosen in ((0, flat), (1, scaled)):
        send_ref[:, half * width : (half + 1) * width] = lax.dot_general(
            chosen,
            held_ref[:, half * width : (half + 1) * width],
            FIRST,
            preferred_element_type=F32,
        ).astype(BF)


def expert_body(
    nblock,
    core_ref,
    came_ref,
    gate_ref,
    up_ref,
    down_ref,
    hidden_ref,
    gate_back_ref,
    up_back_ref,
    route_ref,
    other_ref,
    gate_here,
    up_here,
    back_here,
):
    slots, width = came_ref.shape[0], came_ref.shape[1] // 2
    inputs, scaled = came_ref[:, :width], came_ref[:, width:]
    gate_here[...] = jnp.dot(inputs, gate_ref[...], preferred_element_type=F32)
    up_here[...] = jnp.dot(inputs, up_ref[...], preferred_element_type=F32)
    back_here[...] = lax.dot_general(scaled, down_ref[...], LAST, preferred_element_type=F32)
    step = 32
    for row in range(0, slots, step):
        rows = pl.ds(row, step)
        pre_gate, pre_up, back_hidden = gate_here[rows, :], up_here[rows, :], back_here[rows, :]
        sigma = 1.0 / (1.0 + jnp.exp(-pre_gate))
        active = pre_gate * sigma
        hidden = (active * pre_up).astype(BF)
        hidden_ref[rows, :] = hidden
        gate_back_ref[rows, :] = (
            back_hidden * pre_up * sigma * (1.0 + pre_gate * (1.0 - sigma))
        ).astype(BF)
        up_back_ref[rows, :] = (back_hidden * active).astype(BF)
        route = jnp.sum(hidden.astype(F32) * back_hidden, axis=1, keepdims=True)
        high = route.astype(BF).astype(F32)
        lane = lax.broadcasted_iota(jnp.int32, (step, META), 1)
        route_ref[rows, :] = jnp.where(
            lane == 0, high, jnp.where(lane == 1, route - high, 0.0)
        ).astype(BF)
    for y in range(nblock // 2):
        weight_terms(
            nblock,
            y,
            1 - core_ref[0],
            came_ref,
            hidden_ref[...],
            gate_back_ref[...],
            up_back_ref[...],
            other_ref,
        )


def weight_terms(nblock, y, core, came_ref, hidden, gate_back, up_back, out_ref):
    width = came_ref.shape[1] // 2
    block = width // nblock
    for which, (base, right) in enumerate(((0, gate_back), (0, up_back), (width, hidden))):
        at = pl.multiple_of(base + (2 * y + core) * block, block)
        out_ref[y, which] = lax.dot_general(
            came_ref[:, pl.ds(at, block)], right, FIRST, preferred_element_type=F32
        ).astype(BF)


def own_body(nblock, core_ref, came_ref, hidden_ref, gate_back_ref, up_back_ref, out_ref):
    for y in range(nblock // 2):
        weight_terms(
            nblock,
            y,
            core_ref[0],
            came_ref,
            hidden_ref[...],
            gate_back_ref[...],
            up_back_ref[...],
            out_ref,
        )


def add_body(own_ref, arrived_ref, out_ref, came, went, in_sems, out_sems):
    steps = own_ref.shape[0]
    reads = [
        pltpu.make_async_copy(arrived_ref.at[y], came.at[y], in_sems.at[y]) for y in range(steps)
    ]
    writes = [
        pltpu.make_async_copy(went.at[y], out_ref.at[y], out_sems.at[y]) for y in range(steps)
    ]
    for read in reads:
        read.start()
    for y in range(steps):
        reads[y].wait()
        went[y] = own_ref[y] + came[y]
        writes[y].start()
    for write in writes:
        write.wait()


def final_body(scale, total_ref, gate_ref, up_ref, down_ref):
    block = gate_ref.shape[0]
    gate_ref[...] = total_ref[:block].astype(F32) * scale
    up_ref[...] = total_ref[block : 2 * block].astype(F32) * scale
    down_ref[...] = (total_ref[2 * block :].astype(F32) * scale).T


def sum_body(top, parts_ref, tokens_ref, route_ref):
    width = tokens_ref.shape[1]
    total = parts_ref[0].astype(F32)
    for h in range(1, parts_ref.shape[0]):
        total = total + parts_ref[h].astype(F32)
    tokens_ref[...] = total[:, :width].astype(BF)
    lane = lax.broadcasted_iota(jnp.int32, (top, META), 1)
    row = lax.broadcasted_iota(jnp.int32, (top, META), 0)
    route_ref[...] = lax.dot_general(
        jnp.where(lane == row, 1.0, 0.0).astype(BF),
        total[:, width:].astype(BF),
        LAST,
        preferred_element_type=F32,
    ).astype(BF)


def back_body(gate_back_ref, up_back_ref, route_ref, gate_ref, up_ref, out_ref):
    width = gate_ref.shape[0]
    out = lax.dot_general(gate_back_ref[...], gate_ref[...], LAST, preferred_element_type=F32)
    out = out + lax.dot_general(up_back_ref[...], up_ref[...], LAST, preferred_element_type=F32)
    out_ref[:, :width] = out.astype(BF)
    out_ref[:, width:] = route_ref[...]


def combine_body(top, back_ref, pick_ref, meta_ref, dest_ref, out_ref):
    width = back_ref.shape[1] - META
    pick = pick_ref[...]
    out_ref[:, :width] = jnp.dot(pick, back_ref[:, :width], preferred_element_type=F32).astype(BF)
    lane8 = lax.broadcasted_iota(jnp.int32, (8, META), 1)
    pair = jnp.where(lane8 < 2, 1.0, 0.0).astype(BF)
    route = lax.dot_general(pair, back_ref[:, width:], LAST, preferred_element_type=F32)[0:1]
    mine = jnp.where(pick.astype(F32) > 0.5, route, 0.0)
    meta = meta_ref[...].astype(F32)
    dest = dest_ref[...]
    lane = lax.broadcasted_iota(jnp.int32, (pick.shape[0], META), 1)
    routes = jnp.zeros((pick.shape[0], META), F32)
    for k in range(top):
        value = jnp.sum(
            jnp.where(meta[:, k : k + 1] == dest, mine, 0.0), axis=1, keepdims=True
        )
        routes = jnp.where(lane == k, value / meta[:, top + k : top + k + 1], routes)
    out_ref[:, width:] = routes.astype(BF)


def shards(tokens, expert_ids, route_weights, out_grad, w_gate, w_up, w_down):
    tok, width = tokens.shape
    top = expert_ids.shape[1]
    ff = w_gate.shape[2]
    nx, nh, nl = lax.axis_size("x"), lax.axis_size("zh"), lax.axis_size("zl")
    ny, nc = lax.axis_size("y"), lax.axis_size("core")
    nz = nh * nl
    experts = nx * nz
    cap = min(tok, max(2, 2 * tok * top // experts))
    held = nh * tok
    dests = nx * nl
    per = nh * cap
    slots = dests * per
    nblock = ny * nc
    block = width // nblock

    shift = nl // 2
    groups = [
        [(c * nx + x) * nz + (b * nl + c * shift + l) % nz for x in range(nx) for l in range(nl)]
        for c in range(nc)
        for b in range(nh)
    ]
    core = lax.axis_index("core")
    z = lax.axis_index("zh") * nl + lax.axis_index("zl")
    first = (z - core * shift + nz) % nz // nl * nl + core * shift
    dest = jnp.arange(slots, dtype=jnp.int32) // per
    dest_ids = (dest // nl) * nz + (first + dest % nl) % nz
    dest_ids = dest_ids.astype(F32).reshape(1, slots)
    core_at = core.reshape(1).astype(jnp.int32)

    def forward(a):
        return lax.all_to_all(
            a.reshape(dests, per, -1),
            ("core", "x", "zh", "zl"),
            split_axis=0,
            concat_axis=0,
            tiled=True,
            axis_index_groups=groups,
        ).reshape(slots, -1)

    packed = call(
        functools.partial(pack_body, top),
        jax.ShapeDtypeStruct((tok, 2 * width + META), BF),
        0,
        4 * tok * width,
        ins=[APART] * 4,
        out_specs=APART,
        scratch=[
            pltpu.VMEM((top, tok), jnp.int32),
            pltpu.VMEM((top, tok), BF),
            pltpu.VMEM((tok, META), BF),
            pltpu.SemaphoreType.DMA((5,)),
        ],
        limit=60,
    )(tokens, out_grad, expert_ids.T, route_weights.T)
    gathered = lax.all_gather(packed, "zh", axis=0, tiled=True)

    send, pick, meta = call(
        functools.partial(select_body, tok, cap, top),
        (
            jax.ShapeDtypeStruct((slots, 2 * width), BF),
            jax.ShapeDtypeStruct((held, slots), BF),
            jax.ShapeDtypeStruct((held, META), BF),
        ),
        4 * slots * held * width,
        6 * slots * width,
    )(gathered, dest_ids)
    came = forward(send)

    gate_w, up_w, down_w = w_gate[0], w_up[0], w_down[0]
    small = jax.ShapeDtypeStruct((slots, ff), BF)
    shape = (ny, 3, block, ff)
    terms = jax.ShapeDtypeStruct(shape, BF)
    smem = pl.BlockSpec(memory_space=pltpu.SMEM)
    hidden, gate_back, up_back, route, other = call(
        functools.partial(expert_body, nblock),
        (small, small, small, jax.ShapeDtypeStruct((slots, META), BF), terms),
        9 * slots * ff * width,
        10_000_000,
        ins=[smem] + [VMEM] * 4,
        scratch=[pltpu.VMEM((slots, ff), F32)] * 3,
        limit=28,
        exps=slots * ff,
    )(core_at, came, gate_w, up_w, down_w)
    arrived = lax.ppermute(other, "core", [(0, 1), (1, 0)])
    back = call(
        back_body,
        jax.ShapeDtypeStruct((slots, width + META), BF),
        4 * slots * ff * width,
        5_000_000,
    )(gate_back, up_back, route, gate_w, up_w)
    own = call(
        functools.partial(own_body, nblock),
        terms,
        3 * slots * ff * width,
        5_000_000,
        ins=[smem] + [VMEM] * 4,
    )(core_at, came, hidden, gate_back, up_back)
    own, back = lax.optimization_barrier((own, back))
    pair = call(
        add_body,
        terms,
        0,
        7_000_000,
        ins=[VMEM, APART],
        out_specs=APART,
        scratch=[
            pltpu.VMEM(shape, BF),
            pltpu.VMEM(shape, BF),
            pltpu.SemaphoreType.DMA((ny,)),
            pltpu.SemaphoreType.DMA((ny,)),
        ],
    )(own, arrived)
    total = lax.psum_scatter(
        pair.reshape(ny * 3 * block, ff), "y", scatter_dimension=0, tiled=True
    )
    grads = call(
        functools.partial(final_body, 1.0 / nblock),
        (
            jax.ShapeDtypeStruct((block, ff), F32),
            jax.ShapeDtypeStruct((block, ff), F32),
            jax.ShapeDtypeStruct((ff, block), F32),
        ),
        0,
        9 * block * ff,
        limit=60,
    )(total)

    back = forward(back)
    outgoing = call(
        functools.partial(combine_body, top),
        jax.ShapeDtypeStruct((held, width + META), BF),
        2 * slots * held * width,
        2_000_000,
    )(back, pick, meta, dest_ids)
    parts = lax.all_to_all(
        outgoing.reshape(nh, tok, -1), "zh", split_axis=0, concat_axis=0, tiled=True
    )
    grad_tokens, grad_route = call(
        functools.partial(sum_body, top),
        (jax.ShapeDtypeStruct((tok, width), BF), jax.ShapeDtypeStruct((top, tok), BF)),
        0,
        10 * tok * width,
    )(parts)
    return (grad_tokens, grad_route.T) + tuple(g[None] for g in grads)


def solution(mesh):
    groups, experts = mesh.devices.shape
    n = round(experts ** (1 / 3))
    fine = Mesh(
        mesh.devices.reshape(groups // 2, 2, n, n, n), ("y", "core", "x", "zh", "zl")
    )
    dp = ("y", "core")
    ex = ("x", "zh", "zl")
    rows = P(dp + ex, None)
    return jax.shard_map(
        shards,
        mesh=fine,
        in_specs=(rows, rows, rows, rows) + (P(ex, None, None),) * 3,
        out_specs=(rows, rows, P(ex, dp, None), P(ex, dp, None), P(ex, None, dp)),
        check_vma=False,
    )
```

```python
import functools

import jax
import jax.numpy as jnp
from jax import lax
from jax.experimental import pallas as pl
from jax.experimental.pallas import tpu as pltpu
from jax.sharding import Mesh
from jax.sharding import PartitionSpec as P

BF = jnp.bfloat16
F32 = jnp.float32
META = 128
VMEM = pl.BlockSpec(memory_space=pltpu.VMEM)
APART = pl.BlockSpec(memory_space=pltpu.HBM)
FIRST = (((0,), (0,)), ((), ()))
LAST = (((1,), (1,)), ((), ()))


def call(body, outs, flops, moved, ins=None, scratch=(), limit=16, exps=0, out_specs=None):
    extra = {} if ins is None else {"in_specs": ins}
    if out_specs is not None:
        extra["out_specs"] = out_specs
    return pl.pallas_call(
        body,
        out_shape=outs,
        scratch_shapes=scratch,
        compiler_params=pltpu.CompilerParams(vmem_limit_bytes=limit * 1024 * 1024),
        cost_estimate=pl.CostEstimate(flops=flops, bytes_accessed=moved, transcendentals=exps),
        **extra,
    )


def pack_body(top, tokens_ref, cots_ref, ids_ref, weights_ref, out_ref, ids_here, weights_here, sems):
    width = tokens_ref.shape[1]
    copies = [
        pltpu.make_async_copy(source, target, sems.at[n])
        for n, (source, target) in enumerate(
            (
                (ids_ref, ids_here),
                (weights_ref, weights_here),
                (tokens_ref, out_ref.at[:, pl.ds(0, width)]),
                (cots_ref, out_ref.at[:, pl.ds(width, width)]),
            )
        )
    ]
    for copy in copies:
        copy.start()
    lane = lax.broadcasted_iota(jnp.int32, (top, META), 1)
    row = lax.broadcasted_iota(jnp.int32, (top, META), 0)
    copies[0].wait()
    copies[1].wait()
    meta = lax.dot_general(
        ids_here[...].astype(F32).astype(BF),
        jnp.where(lane == row, 1.0, 0.0).astype(BF),
        FIRST,
        preferred_element_type=F32,
    ) + lax.dot_general(
        weights_here[...].astype(F32).astype(BF),
        jnp.where(lane == row + top, 1.0, 0.0).astype(BF),
        FIRST,
        preferred_element_type=F32,
    )
    out_ref[:, 2 * width :] = meta.astype(BF)
    copies[2].wait()
    copies[3].wait()


def select_body(tok, cap, top, held_ref, dest_ref, send_ref, pick_ref, meta_ref):
    held = held_ref.shape[0]
    slots, width = send_ref.shape[0], send_ref.shape[1] // 2
    meta_ref[...] = held_ref[:, 2 * width :]
    meta = held_ref[:, 2 * width :].astype(F32)
    dest = dest_ref[...]
    match = jnp.zeros((held, slots), F32)
    weight = jnp.zeros((held, slots), F32)
    for k in range(top):
        same = meta[:, k : k + 1] == dest
        match = jnp.where(same, 1.0, match)
        weight = jnp.where(same, meta[:, top + k : top + k + 1], weight)
    row = lax.broadcasted_iota(jnp.int32, (held, held), 0)
    col = lax.broadcasted_iota(jnp.int32, (held, held), 1)
    earlier = jnp.where((col < row) & (col // tok == row // tok), 1.0, 0.0).astype(BF)
    position = jnp.dot(earlier, match.astype(BF), preferred_element_type=F32).astype(jnp.int32)
    token = lax.broadcasted_iota(jnp.int32, (held, slots), 0)
    slot = lax.broadcasted_iota(jnp.int32, (held, slots), 1) % (held // tok * cap)
    pick = (match > 0.5) & (position + token // tok * cap == slot) & (position < cap)
    flat = jnp.where(pick, 1.0, 0.0).astype(BF)
    scaled = jnp.where(pick, weight, 0.0).astype(BF)
    pick_ref[...] = flat
    for half, chosen in ((0, flat), (1, scaled)):
        send_ref[:, half * width : (half + 1) * width] = lax.dot_general(
            chosen,
            held_ref[:, half * width : (half + 1) * width],
            FIRST,
            preferred_element_type=F32,
        ).astype(BF)


def expert_body(
    nblock,
    core_ref,
    came_ref,
    gate_ref,
    up_ref,
    down_ref,
    hidden_ref,
    gate_back_ref,
    up_back_ref,
    route_ref,
    other_ref,
):
    width = came_ref.shape[1] // 2
    inputs, scaled = came_ref[:, :width], came_ref[:, width:]
    pre_gate = jnp.dot(inputs, gate_ref[...], preferred_element_type=F32)
    pre_up = jnp.dot(inputs, up_ref[...], preferred_element_type=F32)
    back_hidden = lax.dot_general(scaled, down_ref[...], LAST, preferred_element_type=F32)
    sigma = 1.0 / (1.0 + jnp.exp(-pre_gate))
    active = pre_gate * sigma
    hidden = (active * pre_up).astype(BF)
    gate_back = (back_hidden * pre_up * sigma * (1.0 + pre_gate * (1.0 - sigma))).astype(BF)
    up_back = (back_hidden * active).astype(BF)
    hidden_ref[...] = hidden
    gate_back_ref[...] = gate_back
    up_back_ref[...] = up_back
    route = jnp.sum(hidden.astype(F32) * back_hidden, axis=1, keepdims=True)
    high = route.astype(BF).astype(F32)
    lane = lax.broadcasted_iota(jnp.int32, route_ref.shape, 1)
    route_ref[...] = jnp.where(
        lane == 0, high, jnp.where(lane == 1, route - high, 0.0)
    ).astype(BF)
    for y in range(nblock // 2):
        weight_terms(nblock, y, 1 - core_ref[0], came_ref, hidden, gate_back, up_back, other_ref)


def weight_terms(nblock, y, core, came_ref, hidden, gate_back, up_back, out_ref):
    width = came_ref.shape[1] // 2
    block = width // nblock
    for which, (base, right) in enumerate(((0, gate_back), (0, up_back), (width, hidden))):
        at = pl.multiple_of(base + (2 * y + core) * block, block)
        out_ref[y, which] = lax.dot_general(
            came_ref[:, pl.ds(at, block)], right, FIRST, preferred_element_type=F32
        ).astype(BF)


def own_body(nblock, core_ref, came_ref, hidden_ref, gate_back_ref, up_back_ref, out_ref):
    for y in range(nblock // 2):
        weight_terms(
            nblock,
            y,
            core_ref[0],
            came_ref,
            hidden_ref[...],
            gate_back_ref[...],
            up_back_ref[...],
            out_ref,
        )


def add_body(own_ref, arrived_ref, out_ref, came, went, in_sems, out_sems):
    steps = own_ref.shape[0]
    reads = [
        pltpu.make_async_copy(arrived_ref.at[y], came.at[y], in_sems.at[y]) for y in range(steps)
    ]
    writes = [
        pltpu.make_async_copy(went.at[y], out_ref.at[y], out_sems.at[y]) for y in range(steps)
    ]
    for read in reads:
        read.start()
    for y in range(steps):
        reads[y].wait()
        went[y] = (own_ref[y].astype(F32) + came[y].astype(F32)).astype(BF)
        writes[y].start()
    for write in writes:
        write.wait()


def final_body(scale, total_ref, gate_ref, up_ref, down_ref):
    block = gate_ref.shape[0]
    gate_ref[...] = total_ref[:block].astype(F32) * scale
    up_ref[...] = total_ref[block : 2 * block].astype(F32) * scale
    down_ref[...] = (total_ref[2 * block :].astype(F32) * scale).T


def sum_body(top, parts_ref, tokens_ref, route_ref):
    width = tokens_ref.shape[1]
    total = parts_ref[0].astype(F32)
    for h in range(1, parts_ref.shape[0]):
        total = total + parts_ref[h].astype(F32)
    tokens_ref[...] = total[:, :width].astype(BF)
    lane = lax.broadcasted_iota(jnp.int32, (top, META), 1)
    row = lax.broadcasted_iota(jnp.int32, (top, META), 0)
    route_ref[...] = lax.dot_general(
        jnp.where(lane == row, 1.0, 0.0).astype(BF),
        total[:, width:].astype(BF),
        LAST,
        preferred_element_type=F32,
    ).astype(BF)


def back_body(gate_back_ref, up_back_ref, route_ref, gate_ref, up_ref, out_ref):
    width = gate_ref.shape[0]
    out = lax.dot_general(gate_back_ref[...], gate_ref[...], LAST, preferred_element_type=F32)
    out = out + lax.dot_general(up_back_ref[...], up_ref[...], LAST, preferred_element_type=F32)
    out_ref[:, :width] = out.astype(BF)
    out_ref[:, width:] = route_ref[...]


def combine_body(top, back_ref, pick_ref, meta_ref, dest_ref, out_ref):
    width = back_ref.shape[1] - META
    pick = pick_ref[...]
    out_ref[:, :width] = jnp.dot(pick, back_ref[:, :width], preferred_element_type=F32).astype(BF)
    lane8 = lax.broadcasted_iota(jnp.int32, (8, META), 1)
    pair = jnp.where(lane8 < 2, 1.0, 0.0).astype(BF)
    route = lax.dot_general(pair, back_ref[:, width:], LAST, preferred_element_type=F32)[0:1]
    mine = jnp.where(pick.astype(F32) > 0.5, route, 0.0)
    meta = meta_ref[...].astype(F32)
    dest = dest_ref[...]
    lane = lax.broadcasted_iota(jnp.int32, (pick.shape[0], META), 1)
    routes = jnp.zeros((pick.shape[0], META), F32)
    for k in range(top):
        value = jnp.sum(
            jnp.where(meta[:, k : k + 1] == dest, mine, 0.0), axis=1, keepdims=True
        )
        routes = jnp.where(lane == k, value / meta[:, top + k : top + k + 1], routes)
    out_ref[:, width:] = routes.astype(BF)


def shards(tokens, expert_ids, route_weights, out_grad, w_gate, w_up, w_down):
    tok, width = tokens.shape
    top = expert_ids.shape[1]
    ff = w_gate.shape[2]
    nx, nh, nl = lax.axis_size("x"), lax.axis_size("zh"), lax.axis_size("zl")
    ny, nc = lax.axis_size("y"), lax.axis_size("core")
    nz = nh * nl
    experts = nx * nz
    cap = min(tok, max(2, 2 * tok * top // experts))
    held = nh * tok
    dests = nx * nl
    per = nh * cap
    slots = dests * per
    nblock = ny * nc
    block = width // nblock

    shift = nl // 2
    groups = [
        [(c * nx + x) * nz + (b * nl + c * shift + l) % nz for x in range(nx) for l in range(nl)]
        for c in range(nc)
        for b in range(nh)
    ]
    groups = [g if n < nh else g[::-1] for n, g in enumerate(groups)]
    core = lax.axis_index("core")
    z = lax.axis_index("zh") * nl + lax.axis_index("zl")
    first = (z - core * shift + nz) % nz // nl * nl + core * shift
    dest = jnp.arange(slots, dtype=jnp.int32) // per
    dest = jnp.where(core == 0, dest, dests - 1 - dest)
    dest_ids = (dest // nl) * nz + (first + dest % nl) % nz
    dest_ids = dest_ids.astype(F32).reshape(1, slots)
    core_at = core.reshape(1).astype(jnp.int32)

    def forward(a):
        return lax.all_to_all(
            a.reshape(dests, per, -1),
            ("core", "x", "zh", "zl"),
            split_axis=0,
            concat_axis=0,
            tiled=True,
            axis_index_groups=groups,
        ).reshape(slots, -1)

    packed = call(
        functools.partial(pack_body, top),
        jax.ShapeDtypeStruct((tok, 2 * width + META), BF),
        0,
        4 * tok * width,
        ins=[APART] * 4,
        out_specs=VMEM,
        scratch=[
            pltpu.VMEM((top, tok), jnp.int32),
            pltpu.VMEM((top, tok), BF),
            pltpu.SemaphoreType.DMA((4,)),
        ],
        limit=60,
    )(tokens, out_grad, expert_ids.T, route_weights.T)
    gathered = lax.all_gather(packed, "zh", axis=0, tiled=True)

    send, pick, meta = call(
        functools.partial(select_body, tok, cap, top),
        (
            jax.ShapeDtypeStruct((slots, 2 * width), BF),
            jax.ShapeDtypeStruct((held, slots), BF),
            jax.ShapeDtypeStruct((held, META), BF),
        ),
        4 * slots * held * width,
        6 * slots * width,
    )(gathered, dest_ids)
    came = forward(send)

    gate_w, up_w, down_w = w_gate[0], w_up[0], w_down[0]
    small = jax.ShapeDtypeStruct((slots, ff), BF)
    shape = (ny, 3, block, ff)
    terms = jax.ShapeDtypeStruct(shape, BF)
    smem = pl.BlockSpec(memory_space=pltpu.SMEM)
    hidden, gate_back, up_back, route, other = call(
        functools.partial(expert_body, nblock),
        (small, small, small, jax.ShapeDtypeStruct((slots, META), BF), terms),
        9 * slots * ff * width,
        10_000_000,
        ins=[smem] + [VMEM] * 4,
        limit=28,
        exps=slots * ff,
    )(core_at, came, gate_w, up_w, down_w)
    arrived = lax.ppermute(other, "core", [(0, 1), (1, 0)])
    back = call(
        back_body,
        jax.ShapeDtypeStruct((slots, width + META), BF),
        4 * slots * ff * width,
        5_000_000,
    )(gate_back, up_back, route, gate_w, up_w)
    own = call(
        functools.partial(own_body, nblock),
        terms,
        3 * slots * ff * width,
        5_000_000,
        ins=[smem] + [VMEM] * 4,
    )(core_at, came, hidden, gate_back, up_back)
    own, back = lax.optimization_barrier((own, back))
    pair = call(
        add_body,
        terms,
        0,
        7_000_000,
        ins=[VMEM, APART],
        out_specs=APART,
        scratch=[
            pltpu.VMEM(shape, BF),
            pltpu.VMEM(shape, BF),
            pltpu.SemaphoreType.DMA((ny,)),
            pltpu.SemaphoreType.DMA((ny,)),
        ],
    )(own, arrived)
    total = lax.psum_scatter(
        pair.reshape(ny * 3 * block, ff), "y", scatter_dimension=0, tiled=True
    )
    grads = call(
        functools.partial(final_body, 1.0 / nblock),
        (
            jax.ShapeDtypeStruct((block, ff), F32),
            jax.ShapeDtypeStruct((block, ff), F32),
            jax.ShapeDtypeStruct((ff, block), F32),
        ),
        0,
        9 * block * ff,
        limit=60,
    )(total)

    back = forward(back)
    outgoing = call(
        functools.partial(combine_body, top),
        jax.ShapeDtypeStruct((held, width + META), BF),
        2 * slots * held * width,
        2_000_000,
    )(back, pick, meta, dest_ids)
    parts = lax.all_to_all(
        outgoing.reshape(nh, tok, -1), "zh", split_axis=0, concat_axis=0, tiled=True
    )
    grad_tokens, grad_route = call(
        functools.partial(sum_body, top),
        (jax.ShapeDtypeStruct((tok, width), BF), jax.ShapeDtypeStruct((top, tok), BF)),
        0,
        10 * tok * width,
    )(parts)
    return (grad_tokens, grad_route.T) + tuple(g[None] for g in grads)


def solution(mesh):
    groups, experts = mesh.devices.shape
    n = round(experts ** (1 / 3))
    fine = Mesh(
        mesh.devices.reshape(groups // 2, 2, n, n, n), ("y", "core", "x", "zh", "zl")
    )
    dp = ("y", "core")
    ex = ("x", "zh", "zl")
    rows = P(dp + ex, None)
    return jax.shard_map(
        shards,
        mesh=fine,
        in_specs=(rows, rows, rows, rows) + (P(ex, None, None),) * 3,
        out_specs=(rows, rows, P(ex, dp, None), P(ex, dp, None), P(ex, None, dp)),
        check_vma=False,
    )
```
